256 devices in a mesh: pb: 32 (over z_hi, y, x), kv: 8 (over z_lo, core).
Axes of the slice: x: 4, y: 4, z: 8 (z_hi: 2, z_lo: 4; z = z_hi * 4 + z_lo), core: 2. Of those that a mesh axis runs over, the one named last changes fastest.
Arguments:
- queries: bfloat16 [32768, 128], P(('kv', 'pb')), may hold values from -7 to 7
- keys: bfloat16 [32768, 128], P(('kv', 'pb')), may hold values from -7 to 7
- values: bfloat16 [32768, 128], P(('kv', 'pb')), may hold values from -6 to 6
- grad_out: bfloat16 [32768, 128], P(('kv', 'pb')), may hold values from -6 to 6
- block_order: int32 [256], replicated, may hold values from 0 to 255, each once
Outputs:
- attn_out: bfloat16 [32768, 128], P(('kv', 'pb'))
- grad_q: bfloat16 [32768, 128], P(('kv', 'pb'))
- grad_k: bfloat16 [32768, 128], P(('kv', 'pb'))
- grad_v: bfloat16 [32768, 128], P(('kv', 'pb'))
The draws below stay inside these ranges and needn't reach their ends.
All inputs are finite; a program needn't handle non-finite values.
Results may differ from the reference program's by a relative error of at most 0.029.
Values may be sent and summed in bfloat16 or wider, within the bound.
A program may use at most 256 MiB of HBM per device.

```python
import jax
import jax.numpy as jnp
from jax import lax

HEAD = 128
TOK_DEV = 128
SHARDS = 256
TOKENS = 32768
N_KV = 8


def draw_queries(key, part):
    key = jax.random.fold_in(key, 1)
    base = jnp.clip(jax.random.normal(key, (TOKENS, HEAD), jnp.float32), -7.0, 7.0)
    return base.astype(jnp.bfloat16)


def draw_keys(key, part):
    key = jax.random.fold_in(key, 2)
    base = jnp.clip(jax.random.normal(key, (TOKENS, HEAD), jnp.float32), -7.0, 7.0)
    return base.astype(jnp.bfloat16)


def level_of(own_key, dims, cuts, low, high):
    loudness = 1.0
    for axis_at, blocks in cuts:
        steps = jax.random.uniform(jax.random.fold_in(jax.random.fold_in(own_key, 6), axis_at), (blocks,), jnp.float32, low / len(cuts), high / len(cuts))
        loudness = loudness * jnp.repeat(jnp.exp(steps), dims[axis_at] // blocks).reshape((-1,) + (1,) * (len(dims) - 1 - axis_at))
    return loudness


def centred(stream_key, shape, width, reach, shards=(), kind=jnp.bfloat16):
    values = width * jax.random.normal(stream_key, shape, jnp.float32)
    if shards:
        values = values * level_of(stream_key, shape, shards, -0.22, 0.18)
    return jnp.clip(values, -reach, reach).astype(kind)


def setup_inputs(seed: int = 0) -> dict:
    streams_of = jax.random.split(jax.random.key(seed), 6)
    queries = draw_queries(jax.random.fold_in(streams_of[5], 71), 0)
    keys = draw_keys(jax.random.fold_in(streams_of[5], 71), 0)
    values = centred(streams_of[2], (TOKENS, HEAD), 1.0, 6.0, ((0, 256),))
    grad_out = centred(streams_of[3], (TOKENS, HEAD), 1.0, 6.0, ((0, 256),))
    block_order = jax.random.permutation(streams_of[4], SHARDS).astype(jnp.int32)
    return {"queries": queries, "keys": keys, "values": values, "grad_out": grad_out, "block_order": block_order}


NEG_BIG = -1.0e30


def positions_of(block_order):
    offsets = jnp.arange(TOK_DEV, dtype=jnp.int32)
    return (block_order[:, None] * TOK_DEV + offsets[None, :]).reshape(-1).astype(jnp.int32)


def reference(queries, keys, values, grad_out, block_order):
    scale = HEAD ** -0.5
    token_pos = positions_of(block_order)
    rows_blk = TOK_DEV * N_KV
    count = TOKENS // rows_blk
    query_blocks = queries.reshape(count, rows_blk, HEAD)
    grad_blocks = grad_out.reshape(count, rows_blk, HEAD)
    pos_blocks = token_pos.reshape(count, rows_blk)

    def forward(inputs):
        query_rows, query_pos = inputs
        scores = jnp.dot(query_rows, keys.T, preferred_element_type=jnp.float32) * scale
        allowed = query_pos[:, None] >= token_pos[None, :]
        rowmax = jnp.max(jnp.where(allowed, scores, NEG_BIG), axis=1)
        weights = jnp.where(allowed, jnp.exp(scores - rowmax[:, None]), 0.0)
        total = jnp.sum(weights, axis=1)
        accum = jnp.dot(weights.astype(jnp.bfloat16), values, preferred_element_type=jnp.float32)
        result = (accum / total[:, None]).astype(jnp.bfloat16)
        return result, rowmax + jnp.log(total)

    out_blocks, lse_blocks = lax.map(forward, (query_blocks, pos_blocks))
    attn_out = out_blocks.reshape(TOKENS, HEAD)
    delta_blocks = jnp.sum(grad_blocks.astype(jnp.float32) * out_blocks.astype(jnp.float32), axis=2)

    def backward(carry, inputs):
        query_rows, grad_rows, query_pos, lse_rows, delta_rows = inputs
        scores = jnp.dot(query_rows, keys.T, preferred_element_type=jnp.float32) * scale
        allowed = query_pos[:, None] >= token_pos[None, :]
        probs = jnp.where(allowed, jnp.exp(scores - lse_rows[:, None]), 0.0)
        probs_b = probs.astype(jnp.bfloat16)
        dprobs = jnp.dot(grad_rows, values.T, preferred_element_type=jnp.float32)
        dscores = (probs * (dprobs - delta_rows[:, None])).astype(jnp.bfloat16)
        grad_rows_q = jnp.dot(dscores, keys, preferred_element_type=jnp.float32) * scale
        grad_keys = jnp.dot(dscores.T, query_rows, preferred_element_type=jnp.float32) * scale
        grad_vals = jnp.dot(probs_b.T, grad_rows, preferred_element_type=jnp.float32)
        return (carry[0] + grad_keys, carry[1] + grad_vals), grad_rows_q

    start = (jnp.zeros((TOKENS, HEAD), jnp.float32), jnp.zeros((TOKENS, HEAD), jnp.float32))
    sums, grad_q_blocks = lax.scan(backward, start, (query_blocks, grad_blocks, pos_blocks, lse_blocks, delta_blocks))
    grad_q = grad_q_blocks.reshape(TOKENS, HEAD).astype(jnp.bfloat16)
    return attn_out, grad_q, sums[0].astype(jnp.bfloat16), sums[1].astype(jnp.bfloat16)
```

```python
import functools

import jax
import jax.numpy as jnp
from jax import lax
from jax.experimental import pallas as pl
from jax.experimental.pallas import tpu as pltpu
from jax.sharding import PartitionSpec as P

MESH = pl.DeviceIdType.MESH
F32 = jnp.float32
BF16 = jnp.bfloat16
BIG = 1e30
B = 128
G = 16
N = B * G
CH = 256
STEPS = N // CH


def dot(left, right, left_dim, right_dim):
    return lax.dot_general(
        left, right, (((left_dim,), (right_dim,)), ((), ())), preferred_element_type=F32
    )


def split3(row):
    first = row.astype(BF16).astype(F32)
    second = (row - first).astype(BF16).astype(F32)
    return [first, second, row - first - second]


def kernel(
    q_ref, k_ref, v_ref, g_ref, order_ref,
    out_ref, dq_ref, dk_ref, dv_ref,
    qg, kvg, kt, vt, bias, tri, stats, probs, dprobs, dsc, o_send, o_recv, st_send, st_recv,
    qs, gs, dq_send, dq_recv, kv_send, kv_recv, ssem, rsem,
):
    scale = B ** -0.5
    log_scale = scale * 1.4426950408889634
    pb, kv = lax.axis_index("pb"), lax.axis_index("kv")
    place = lax.rem(pb, 16)
    x, y = lax.rem(place, 4), place // 4
    z_hi = pb // 16
    z, core = z_hi * 4 + kv // 2, lax.rem(kv, 2)

    def line_peer(slot, sign):
        to_z = lax.rem(z + 8 + sign * (slot // 2), 8)
        to_core = lax.rem(core + lax.rem(slot, 2), 2)
        return (to_z // 4) * 16 + place, lax.rem(to_z, 4) * 2 + to_core

    def plane_peer(slot, sign):
        to_x = lax.rem(x + 4 + sign * lax.rem(slot, 4), 4)
        to_y = lax.rem(y + 4 + sign * (slot // 4), 4)
        return z_hi * 16 + to_y * 4 + to_x, kv

    def copy(kind, src, dst, slot, peer):
        return pltpu.make_async_remote_copy(
            src_ref=src, dst_ref=dst, send_sem=ssem.at[kind, slot], recv_sem=rsem.at[kind, slot],
            device_id=peer, device_id_type=MESH,
        )

    barrier = pltpu.get_barrier_semaphore()

    def greet(slot, carry):
        for peer in (line_peer(slot, 1), plane_peer(slot, 1)):
            pl.semaphore_signal(barrier, inc=1, device_id=peer, device_id_type=MESH)
        return carry

    lax.fori_loop(1, G, greet, 0)
    qg[0, 0] = q_ref[...].T
    qg[0, 1] = g_ref[...].T
    kvg[0, 0] = k_ref[...]
    kvg[0, 1] = v_ref[...]
    pl.semaphore_wait(barrier, 2 * (G - 1))

    def gather_q(slot):
        return copy(0, qg.at[0], qg.at[slot], slot, line_peer(slot, 1))

    def gather_kv(slot):
        return copy(1, kvg.at[0], kvg.at[slot], slot, plane_peer(slot, 1))

    def send_o(slot):
        return copy(2, o_send.at[slot], o_recv.at[slot], slot, line_peer(slot, -1))

    def send_st(slot):
        return copy(3, st_send, st_recv.at[slot], slot, line_peer(slot, 1))

    def send_dq(slot):
        return copy(4, dq_send.at[slot], dq_recv.at[slot], slot, line_peer(slot, -1))

    def send_kv(slot):
        return copy(5, kv_send.at[slot], kv_recv.at[slot], slot, plane_peer(slot, -1))

    def over_slots(*steps):
        def one(slot, carry):
            for step in steps:
                step(slot)
            return carry

        lax.fori_loop(1, G, one, 0)

    over_slots(lambda s: gather_q(s).start(), lambda s: gather_kv(s).start())

    lane = lax.broadcasted_iota(jnp.int32, (B, B), 1)
    sub = lax.broadcasted_iota(jnp.int32, (B, B), 0)
    tri[...] = jnp.zeros_like(tri)
    tri[:, 0:B] = jnp.where(sub > lane, -BIG, 0.0)
    q_pos = []
    for slot in range(G):
        to_pb, to_kv = line_peer(slot, -1)
        q_pos.append(jnp.full((1, B), order_ref[to_kv * 32 + to_pb], jnp.int32))
    q_pos = jnp.concatenate(q_pos, axis=1)
    for slot in range(G):
        to_pb, to_kv = plane_peer(slot, -1)
        bias[slot : slot + 1, :] = jnp.where(order_ref[to_kv * 32 + to_pb] > q_pos, BIG, 0.0)

    over_slots(lambda s: gather_kv(s).wait_recv())

    def turn(slot, carry):
        at = pl.ds(pl.multiple_of(slot * B, B), B)
        kt[:, at] = kvg[slot, 0].T
        vt[:, at] = kvg[slot, 1].T
        return carry

    lax.fori_loop(0, G, turn, 0)
    over_slots(lambda s: gather_q(s).wait_recv())

    def keys():
        return kvg[:, 0].reshape(N, B)

    def values():
        return kvg[:, 1].reshape(N, B)

    def pair(ref, step, which):
        return jnp.concatenate([ref[2 * step, which], ref[2 * step + 1, which]], axis=1)

    def forward(step, carry):
        at = pl.ds(pl.multiple_of(step * CH, CH), CH)
        s = dot(keys(), pair(qg, step, 0), 1, 0).reshape(G, B, CH)
        s = jnp.concatenate([s[0:1] + tri[:, at][None], s[1:]], axis=0)
        off = bias[:, at]
        rowmax = jnp.max(jnp.where(off > 0, -BIG, jnp.max(s, axis=1)), axis=0, keepdims=True)
        shift = jnp.where(off > 0, BIG, rowmax)
        p = jnp.exp2((s - shift[:, None, :]) * log_scale).reshape(N, CH)
        total = jnp.sum(p, axis=0, keepdims=True)
        p = p.astype(BF16)
        probs[:, at] = p
        stats[0:1, at] = rowmax
        accum = dot(vt[...], p, 1, 0)
        rows = split3(rowmax) + split3(total) + [jnp.zeros((10, CH), F32)]
        packed = jnp.concatenate([accum] + rows, axis=0).astype(BF16)
        for half in range(2):
            o_send[2 * step + half] = packed[:, half * B : (half + 1) * B]
        return carry

    lax.fori_loop(0, STEPS, forward, 0)
    over_slots(lambda s: send_o(s).start())

    def dprob(step, carry):
        at = pl.ds(pl.multiple_of(step * CH, CH), CH)
        dprobs[:, at] = dot(values(), pair(qg, step, 1), 1, 0)
        return carry

    lax.fori_loop(0, STEPS, dprob, 0)

    o_recv[0] = o_send[0]
    over_slots(lambda s: send_o(s).wait_recv())
    tail = o_recv[:, B : B + 16].astype(F32)
    maxes = tail[:, 0:1] + tail[:, 1:2] + tail[:, 2:3]
    totals = tail[:, 3:4] + tail[:, 4:5] + tail[:, 5:6]
    top = jnp.max(maxes, axis=0, keepdims=True)
    factor = jnp.exp2((maxes - top) * log_scale)
    whole = jnp.sum(totals * factor, axis=0)
    accum = jnp.zeros((B, B), F32)
    for slot in range(G):
        accum += o_recv[slot, 0:B].astype(F32) * factor[slot]
    out_t = (accum / whole).astype(BF16)
    out_ref[...] = out_t.T
    delta = jnp.sum(qg[0, 1].astype(F32) * out_t.astype(F32), axis=0, keepdims=True)
    lse = top[0] * log_scale + jnp.log2(whole)
    st_send[...] = jnp.concatenate([lse, delta, jnp.zeros((6, B), F32)], axis=0)
    over_slots(lambda s: send_st(s).start())
    st_recv[0] = st_send[...]
    over_slots(lambda s: send_st(s).wait_recv())

    def rescale(slot, carry):
        at = pl.ds(pl.multiple_of(slot * B, B), B)
        weight = jnp.exp2(stats[0:1, at] * log_scale - st_recv[slot, 0:1])
        stats[1:2, at] = st_recv[slot, 1:2]
        stats[2:3, at] = weight * scale
        qs[:, at] = (qg[slot, 0].astype(F32) * weight).astype(BF16)
        gs[:, at] = (qg[slot, 1].astype(F32) * weight).astype(BF16)
        return carry

    lax.fori_loop(0, G, rescale, 0)

    def backward_q(step, carry):
        at = pl.ds(pl.multiple_of(step * CH, CH), CH)
        ds = (probs[:, at].astype(F32) * (dprobs[:, at] - stats[1:2, at])).astype(BF16)
        dsc[:, at] = ds
        terms = (dot(kt[...], ds, 1, 0) * stats[2:3, at]).astype(BF16)
        for half in range(2):
            dq_send[2 * step + half] = terms[:, half * B : (half + 1) * B]
        return carry

    lax.fori_loop(0, STEPS, backward_q, 0)
    over_slots(lambda s: send_dq(s).start())

    def backward_kv(step, carry):
        at = pl.ds(pl.multiple_of(step * CH, CH), CH)
        key_terms = (dot(dsc[at, :], qs[...], 1, 1) * scale).astype(BF16)
        value_terms = dot(probs[at, :], gs[...], 1, 1).astype(BF16)
        for half in range(2):
            kv_send[2 * step + half, 0] = key_terms[half * B : (half + 1) * B]
            kv_send[2 * step + half, 1] = value_terms[half * B : (half + 1) * B]
        return carry

    lax.fori_loop(0, STEPS, backward_kv, 0)
    over_slots(lambda s: send_kv(s).start())

    dq_recv[0] = dq_send[0]
    over_slots(lambda s: send_dq(s).wait_recv())
    dq_ref[...] = jnp.sum(dq_recv[...].astype(F32), axis=0).astype(BF16).T
    kv_recv[0] = kv_send[0]
    over_slots(lambda s: send_kv(s).wait_recv())
    dk_ref[...] = jnp.sum(kv_recv[:, 0].astype(F32), axis=0).astype(BF16)
    dv_ref[...] = jnp.sum(kv_recv[:, 1].astype(F32), axis=0).astype(BF16)
    over_slots(*[lambda s, f=f: f(s).wait_send() for f in (gather_q, gather_kv, send_o, send_st, send_dq, send_kv)])


def per_device(queries, keys, values, grad_out, block_order):
    vmem = pl.BlockSpec(memory_space=pltpu.VMEM)
    block = jax.ShapeDtypeStruct((B, B), BF16)
    return pl.pallas_call(
        kernel,
        out_shape=[block] * 4,
        in_specs=[vmem] * 4 + [pl.BlockSpec(memory_space=pltpu.SMEM)],
        out_specs=[vmem] * 4,
        scratch_shapes=[
            pltpu.VMEM((G, 2, B, B), BF16),
            pltpu.VMEM((G, 2, B, B), BF16),
            pltpu.VMEM((B, N), BF16),
            pltpu.VMEM((B, N), BF16),
            pltpu.VMEM((G, N), F32),
            pltpu.VMEM((B, N), F32),
            pltpu.VMEM((8, N), F32),
            pltpu.VMEM((N, N), BF16),
            pltpu.VMEM((N, N), F32),
            pltpu.VMEM((N, N), BF16),
            pltpu.VMEM((G, B + 16, B), BF16),
            pltpu.VMEM((G, B + 16, B), BF16),
            pltpu.VMEM((8, B), F32),
            pltpu.VMEM((G, 8, B), F32),
            pltpu.VMEM((B, N), BF16),
            pltpu.VMEM((B, N), BF16),
            pltpu.VMEM((G, B, B), BF16),
            pltpu.VMEM((G, B, B), BF16),
            pltpu.VMEM((G, 2, B, B), BF16),
            pltpu.VMEM((G, 2, B, B), BF16),
            pltpu.SemaphoreType.DMA((6, G)),
            pltpu.SemaphoreType.DMA((6, G)),
        ],
        compiler_params=pltpu.CompilerParams(
            collective_id=0, has_side_effects=True, vmem_limit_bytes=60 * 2**20
        ),
        name="attention",
    )(queries, keys, values, grad_out, block_order)


def solution(mesh):
    spec = P(("kv", "pb"), None)
    return jax.shard_map(
        per_device, mesh=mesh, in_specs=(spec, spec, spec, spec, P()), out_specs=(spec,) * 4,
        check_vma=False,
    )
```

```python
import jax
import jax.numpy as jnp
from jax import lax
from jax.experimental import pallas as pl
from jax.experimental.pallas import tpu as pltpu
from jax.sharding import PartitionSpec as P

MESH = pl.DeviceIdType.MESH
F32 = jnp.float32
BF16 = jnp.bfloat16
BIG = 1e30
TINY = 1e-30
B = 128
ZQ = 8
NQ = ZQ * B
CHUNKS = 8
KC = 4 * B
CQ = 2 * B
Q_AT, KV_AT, FWD_AT, ST_AT, O_AT, PRE_AT, BACK_AT, DQ_AT, SEMS = 0, 8, 24, 28, 36, 44, 48, 64, 72


def dot(left, right, left_dim, right_dim):
    return lax.dot_general(
        left, right, (((left_dim,), (right_dim,)), ((), ())), preferred_element_type=F32
    )


def ring4(code):
    return code + code // 2 - 2 * (code // 3)


def ring8(code):
    odd = lax.rem(code, 2)
    return odd * ((code + 1) // 2) + (1 - odd) * lax.rem(8 - code // 2, 8)


def kernel(
    q_ref, k_ref, v_ref, g_ref, order_ref,
    out_ref, dq_ref, dk_ref, dv_ref,
    qg, kvg, kt, vt, bias, maxes, totals, deltas, factors, rows, probs, dprobs, dsc,
    st_send, st_recv, o_send, o_recv, pre_send, pre_recv, part, back_send, back_recv, dq_sum, dq_send, dq_recv,
    ssem, rsem,
):
    scale = B ** -0.5
    log_scale = scale * 1.4426950408889634
    pb, kv = lax.axis_index("pb"), lax.axis_index("kv")
    place = lax.rem(pb, 16)
    x, y = lax.rem(place, 4), place // 4
    z_hi = pb // 16
    z, core = z_hi * 4 + kv // 2, lax.rem(kv, 2)

    def line_z(code, sign):
        return lax.rem(z + 8 + sign * ring8(code), 8)

    def line(code, sign):
        to_z = line_z(code, sign)
        return (to_z // 4) * 16 + place, lax.rem(to_z, 4) * 2 + core

    def plane(slot, sign):
        to_x = lax.rem(x + 4 + sign * ring4(lax.rem(slot, 4)), 4)
        to_y = lax.rem(y + 4 + sign * ring4(slot // 4), 4)
        return z_hi * 16 + to_y * 4 + to_x, kv

    sibling = (pb, (kv // 2) * 2 + 1 - core)

    def copy(src, dst, sem, peer):
        return pltpu.make_async_remote_copy(
            src_ref=src, dst_ref=dst, send_sem=ssem.at[sem], recv_sem=rsem.at[sem],
            device_id=peer, device_id_type=MESH,
        )

    def gather_q(i):
        return copy(qg.at[0], qg.at[i], Q_AT + i, line(i, 1))

    def gather_kv(s):
        return copy(kvg.at[0, 0], kvg.at[2 * (s // 4), lax.rem(s, 4)], KV_AT + s, plane(s, 1))

    def forward_kv(t):
        return copy(kvg.at[2 * t], kvg.at[2 * t + 1], FWD_AT + t, sibling)

    def send_st(i):
        return copy(st_send, st_recv.at[z], ST_AT + i, line(i, 1))

    def send_o(i):
        return copy(o_send.at[i], o_recv.at[i], O_AT + i, line(i, -1))

    def send_pre(t):
        return copy(pre_send.at[t], pre_recv.at[t], PRE_AT + t, sibling)

    def send_back(s):
        return copy(back_send.at[s], back_recv.at[s], BACK_AT + s, plane(s, -1))

    def send_dq(i):
        return copy(dq_send.at[i], dq_recv.at[i], DQ_AT + i, line(i, -1))

    def loop(start, stop, *steps):
        def one(i, carry):
            for step in steps:
                step(i)
            return carry

        lax.fori_loop(start, stop, one, 0)

    barrier = pltpu.get_barrier_semaphore()

    def greet(peer):
        pl.semaphore_signal(barrier, inc=1, device_id=peer, device_id_type=MESH)

    loop(1, 16, lambda s: greet(plane(s, 1)))
    loop(1, ZQ, lambda i: greet(line(i, 1)))
    greet(sibling)
    qg[0, 0] = q_ref[...].T
    qg[0, 1] = g_ref[...].T
    kvg[0, 0, 0] = k_ref[...]
    kvg[0, 0, 1] = v_ref[...]
    pl.semaphore_wait(barrier, 15 + ZQ)
    loop(1, ZQ, lambda i: gather_q(i).start(), lambda i: gather_kv(i).start())
    loop(ZQ, 16, lambda s: gather_kv(s).start())

    q_pos = []
    for i in range(ZQ):
        at_pb, at_kv = line(i, -1)
        q_pos.append(jnp.full((1, B), order_ref[at_kv * 32 + at_pb], jnp.int32))
    q_pos = jnp.concatenate(q_pos, axis=1)
    for s in range(16):
        at_pb, at_kv = plane(s, -1)
        for r in range(2):
            k_pos = order_ref[(at_kv + r * (1 - 2 * core)) * 32 + at_pb]
            j, b = 2 * (s // 4) + r, s % 4
            bias[j, b : b + 1, :] = jnp.where(k_pos > q_pos, BIG, 0.0)

    def pair(ref, i, which):
        return jnp.concatenate([ref[2 * i, which], ref[2 * i + 1, which]], axis=1)

    def tile(j, i, own=False):
        at = pl.ds(pl.multiple_of(i * CQ, CQ), CQ)
        s = dot(kvg[j, :, 0].reshape(KC, B), pair(qg, i, 0), 1, 0).reshape(4, B, CQ)
        if own:
            lane = lax.broadcasted_iota(jnp.int32, (B, CQ), 1)
            sub = lax.broadcasted_iota(jnp.int32, (B, CQ), 0)
            later = jnp.where((sub > lane) & (lane < B), -BIG, 0.0)
            s = jnp.concatenate([s[0:1] + later[None], s[1:]], axis=0)
        off = bias[j, :, at] > 0
        rowmax = jnp.max(jnp.where(off, -BIG, jnp.max(s, axis=1)), axis=0, keepdims=True)
        shift = jnp.where(off, BIG, rowmax)
        p = jnp.exp2((s - shift[:, None, :]) * log_scale).reshape(KC, CQ)
        dp = dot(kvg[j, :, 1].reshape(KC, B), pair(qg, i, 1), 1, 0)
        one = pl.ds(j, 1)
        maxes[one, at] = rowmax
        totals[one, at] = jnp.sum(p, axis=0, keepdims=True)
        deltas[one, at] = jnp.sum(p * dp, axis=0, keepdims=True)
        probs[j, :, at] = p.astype(BF16)
        dprobs[j, :, at] = dp

    for t in range(4):
        loop(max(4 * t, 1), 4 * t + 4, lambda s: gather_kv(s).wait_recv())
        forward_kv(t).start()
        loop(max(2 * t, 1), 2 * t + 2, lambda i: gather_q(i).wait_recv())
        if t == 0:
            tile(0, 0, own=True)
        else:
            loop(0, t + 1, lambda i: tile(2 * t, i))
            loop(0, 2 * t, lambda j: tile(j, t))
        forward_kv(t).wait_recv()
        loop(0, t + 1, lambda i: tile(2 * t + 1, i))

    top = jnp.max(maxes[...], axis=0, keepdims=True)
    factor = jnp.exp2((maxes[...] - top) * log_scale)
    total = jnp.maximum(jnp.sum(factor * totals[...], axis=0, keepdims=True), TINY)
    near = top * log_scale + jnp.log2(total)
    mean = jnp.sum(factor * deltas[...], axis=0, keepdims=True) / total
    factors[...] = factor / total
    for i in range(ZQ):
        one = pl.ds(line_z(i, -1), 1)
        st_send[0, one, :] = near[:, i * B : (i + 1) * B]
        st_send[1, one, :] = mean[:, i * B : (i + 1) * B]
    loop(1, ZQ, lambda i: send_st(i).start())
    st_recv[z] = st_send[...]

    def turn(j):
        kt[j] = kvg[j, :, 0].reshape(KC, B).T
        vt[j] = kvg[j, :, 1].reshape(KC, B).T

    loop(0, CHUNKS, turn)

    def attend(i):
        at = pl.ds(pl.multiple_of(i * CQ, CQ), CQ)
        accum = jnp.zeros((B, CQ), F32)
        for j in range(CHUNKS):
            accum += dot(vt[j], probs[j, :, at], 1, 0) * factors[j : j + 1, at]
        accum = accum.astype(BF16)
        o_send[2 * i] = accum[:, :B]
        o_send[2 * i + 1] = accum[:, B:]

    loop(0, ZQ // 2, attend)
    loop(1, ZQ, lambda i: send_o(i).start())
    o_recv[0] = o_send[0]

    loop(1, ZQ, lambda i: send_st(i).wait_recv())
    nears, means = st_recv[:, 0], st_recv[:, 1]
    top = jnp.max(nears, axis=0)
    lse = top + jnp.log2(jnp.sum(jnp.exp2(nears - top[None]), axis=0))
    delta = jnp.sum(jnp.exp2(nears - lse[None]) * means, axis=0)
    rows[0:8, :] = lse
    rows[8:16, :] = delta
    lse_row = jnp.concatenate([rows[pl.ds(line_z(i, -1), 1), :] for i in range(ZQ)], axis=1)
    delta_row = jnp.concatenate([rows[pl.ds(8 + line_z(i, -1), 1), :] for i in range(ZQ)], axis=1)
    maxes[...] = jnp.exp2(maxes[...] * log_scale - lse_row)
    deltas[0:1, :] = delta_row
    dq_sum[...] = jnp.zeros_like(dq_sum)

    def whole(which):
        return jnp.concatenate([qg[i, which] for i in range(ZQ)], axis=1)

    def backward(j):
        for i in range(NQ // CQ):
            at = slice(i * CQ, (i + 1) * CQ)
            p = probs[j, :, at].astype(F32) * maxes[pl.ds(j, 1), at]
            probs[j, :, at] = p.astype(BF16)
            dsc[:, at] = (p * (dprobs[j, :, at] - deltas[0:1, at])).astype(BF16)
        dk = dot(dsc[...], whole(0), 1, 1) * scale
        dv = dot(probs[j], whole(1), 1, 1)
        dq_sum[...] += dot(kt[j], dsc[...], 1, 0)
        return dk.reshape(4, B, B), dv.reshape(4, B, B)

    def merge(t):
        send_pre(t).wait_recv()
        both = (part[t].astype(F32) + pre_recv[t].astype(F32)).astype(BF16)
        back_send[pl.ds(4 * t, 4)] = both
        loop(jnp.maximum(4 * t, 1), 4 * t + 4, lambda s: send_back(s).start())

    def backward_pair(n):
        t = 3 - n
        dk, dv = backward(2 * t + 1)
        pre_send[t, :, 0] = dk.astype(BF16)
        pre_send[t, :, 1] = dv.astype(BF16)
        send_pre(t).start()
        dk, dv = backward(2 * t)
        part[t, :, 0] = dk
        part[t, :, 1] = dv
        merge(t)

    loop(0, 4, backward_pair)
    terms = (dq_sum[...] * scale).astype(BF16)
    for i in range(ZQ):
        dq_send[i] = terms[:, i * B : (i + 1) * B]
    loop(1, ZQ, lambda i: send_dq(i).start())

    loop(1, ZQ, lambda i: send_o(i).wait_recv())
    out = jnp.zeros((B, B), F32)
    for i in range(ZQ):
        weight = jnp.exp2(st_recv[line_z(i, 1), 0, pl.ds(z, 1), :] - rows[pl.ds(z, 1), :])
        out += o_recv[i].astype(F32) * weight
    out_ref[...] = out.astype(BF16).T
    dq_recv[0] = dq_send[0]
    loop(1, ZQ, lambda i: send_dq(i).wait_recv())
    dq_ref[...] = jnp.sum(dq_recv[...].astype(F32), axis=0).astype(BF16).T
    back_recv[0] = back_send[0]
    loop(1, 16, lambda s: send_back(s).wait_recv())
    dk_ref[...] = jnp.sum(back_recv[:, 0].astype(F32), axis=0).astype(BF16)
    dv_ref[...] = jnp.sum(back_recv[:, 1].astype(F32), axis=0).astype(BF16)
    loop(1, ZQ, *[lambda i, f=f: f(i).wait_send() for f in (gather_q, send_st, send_o, send_dq)])
    loop(1, 16, *[lambda s, f=f: f(s).wait_send() for f in (gather_kv, send_back)])
    loop(0, 4, *[lambda t, f=f: f(t).wait_send() for f in (forward_kv, send_pre)])


def per_device(queries, keys, values, grad_out, block_order):
    vmem = pl.BlockSpec(memory_space=pltpu.VMEM)
    block = jax.ShapeDtypeStruct((B, B), BF16)
    return pl.pallas_call(
        kernel,
        out_shape=[block] * 4,
        in_specs=[vmem] * 4 + [pl.BlockSpec(memory_space=pltpu.SMEM)],
        out_specs=[vmem] * 4,
        scratch_shapes=[
            pltpu.VMEM((ZQ, 2, B, B), BF16),
            pltpu.VMEM((CHUNKS, 4, 2, B, B), BF16),
            pltpu.VMEM((CHUNKS, B, KC), BF16),
            pltpu.VMEM((CHUNKS, B, KC), BF16),
            pltpu.VMEM((CHUNKS, 4, NQ), F32),
            pltpu.VMEM((CHUNKS, NQ), F32),
            pltpu.VMEM((CHUNKS, NQ), F32),
            pltpu.VMEM((CHUNKS, NQ), F32),
            pltpu.VMEM((CHUNKS, NQ), F32),
            pltpu.VMEM((16, B), F32),
            pltpu.VMEM((CHUNKS, KC, NQ), BF16),
            pltpu.VMEM((CHUNKS, KC, NQ), F32),
            pltpu.VMEM((KC, NQ), BF16),
            pltpu.VMEM((2, 8, B), F32),
            pltpu.VMEM((ZQ, 2, 8, B), F32),
            pltpu.VMEM((ZQ, B, B), BF16),
            pltpu.VMEM((ZQ, B, B), BF16),
            pltpu.VMEM((4, 4, 2, B, B), BF16),
            pltpu.VMEM((4, 4, 2, B, B), BF16),
            pltpu.VMEM((4, 4, 2, B, B), F32),
            pltpu.VMEM((16, 2, B, B), BF16),
            pltpu.VMEM((16, 2, B, B), BF16),
            pltpu.VMEM((B, NQ), F32),
            pltpu.VMEM((ZQ, B, B), BF16),
            pltpu.VMEM((ZQ, B, B), BF16),
            pltpu.SemaphoreType.DMA((SEMS,)),
            pltpu.SemaphoreType.DMA((SEMS,)),
        ],
        compiler_params=pltpu.CompilerParams(
            collective_id=0, has_side_effects=True, vmem_limit_bytes=60 * 2**20
        ),
        name="attention",
    )(queries, keys, values, grad_out, block_order)


def solution(mesh):
    spec = P(("kv", "pb"), None)
    return jax.shard_map(
        per_device, mesh=mesh, in_specs=(spec, spec, spec, spec, P()), out_specs=(spec,) * 4,
        check_vma=False,
    )
```

```python
import jax
import jax.numpy as jnp
from jax import lax
from jax.experimental import pallas as pl
from jax.experimental.pallas import tpu as pltpu
from jax.sharding import PartitionSpec as P

MESH = pl.DeviceIdType.MESH
F32 = jnp.float32
BF16 = jnp.bfloat16
BIG = 1e30
TINY = 1e-30
B = 128
ZQ = 8
NQ = ZQ * B
CHUNKS = 8
KC = 4 * B
CQ = 2 * B
RING4 = (0, 1, 3, 2)
RING8 = (0, 1, 7, 2, 6, 3, 5, 4)


class Sems:
    def __init__(self):
        self.count = 0

    def take(self):
        self.count += 1
        return self.count - 1


SEMS = 82

def dot(left, right, left_dim, right_dim):
    return lax.dot_general(
        left, right, (((left_dim,), (right_dim,)), ((), ())), preferred_element_type=F32
    )


def kernel(
    q_ref, k_ref, v_ref, g_ref, order_ref,
    out_ref, dq_ref, dk_ref, dv_ref,
    qg, kvg, kt, vt, bias, maxes, totals, deltas, factors, rows, probs, dprobs, dscores,
    st_send, st_recv, o_send, o_recv, dq_send, dq_recv, pre_send, pre_recv, part,
    dk_row, dk_got, dk_turn, dk_last, dv_col, dv_got, dv_turn, dv_last,
    ssem, rsem,
):
    scale = B ** -0.5
    log_scale = scale * 1.4426950408889634
    pb, kv = lax.axis_index("pb"), lax.axis_index("kv")
    place = lax.rem(pb, 16)
    x, y = lax.rem(place, 4), place // 4
    z_hi = pb // 16
    z, core = z_hi * 4 + kv // 2, lax.rem(kv, 2)

    xs = [lax.rem(x + d, 4) for d in range(4)]
    ys = [lax.rem(y + d, 4) for d in range(4)]
    zs = [lax.rem(z + d, 8) for d in range(8)]
    pb_z = [at // 4 * 16 + place for at in zs]
    kv_z = [lax.rem(at, 4) * 2 + core for at in zs]

    def row(dx):
        return (z_hi * 16 + y * 4 + xs[dx % 4], kv)

    def column(dy):
        return (z_hi * 16 + ys[dy % 4] * 4 + x, kv)

    def line(dz):
        return (pb_z[dz % 8], kv_z[dz % 8])

    sibling = (pb, kv + 1 - 2 * core)
    sems = Sems()

    def copy(src, dst, peer):
        at = sems.take()
        return pltpu.make_async_remote_copy(
            src_ref=src, dst_ref=dst, send_sem=ssem.at[at], recv_sem=rsem.at[at],
            device_id=peer, device_id_type=MESH,
        )

    sent = []

    def start(copies):
        for one in copies:
            one.start()
            sent.append(one)

    def arrived(copies):
        for one in copies:
            one.wait_recv()

    barrier = pltpu.get_barrier_semaphore()
    peers = [line(d) for d in range(1, 8)] + [f(d) for f in (row, column) for d in (1, 2, 3)] + [sibling]
    for peer in peers:
        pl.semaphore_signal(barrier, inc=1, device_id=peer, device_id_type=MESH)
    qg[0, 0] = q_ref[...].T
    qg[0, 1] = g_ref[...].T
    kvg[0, 0, 0, 0] = k_ref[...]
    kvg[0, 0, 1, 0] = v_ref[...]
    pl.semaphore_wait(barrier, len(peers))

    k_row = {b: copy(kvg.at[0, 0, 0, 0], kvg.at[0, 0, 0, b], row(RING4[b])) for b in (1, 2, 3)}
    v_col = {t: copy(kvg.at[0, 0, 1, 0], kvg.at[t, 0, 1, 0], column(RING4[t])) for t in (1, 2, 3)}
    q_near = {i: copy(qg.at[0], qg.at[i], line(RING8[i])) for i in (3, 4, 1, 2)}
    k_col = {t: copy(kvg.at[0, 0, 0, 0], kvg.at[t, 0, 0, 0], column(RING4[t])) for t in (1, 2, 3)}
    v_row = {b: copy(kvg.at[0, 0, 1, 0], kvg.at[0, 0, 1, b], row(RING4[b])) for b in (1, 2, 3)}
    k_on = {t: copy(kvg.at[0, 0, 0, pl.ds(1, 3)], kvg.at[t, 0, 0, pl.ds(1, 3)], column(RING4[t])) for t in (1, 2, 3)}
    v_on = {
        t: [copy(kvg.at[t, 0, 1, 0], kvg.at[t, 0, 1, b], row(RING4[b])) for b in (1, 2, 3)] for t in (1, 2, 3)
    }
    q_on = {
        5: [copy(qg.at[3], qg.at[5], line(1))],
        6: [copy(qg.at[4], qg.at[6], line(-1))],
        7: [copy(qg.at[3, 0], qg.at[7, 0], line(2)), copy(qg.at[4, 1], qg.at[7, 1], line(-2))],
    }
    share = [copy(kvg.at[t, 0], kvg.at[t, 1], sibling) for t in range(4)]

    start(k_row.values())
    start(v_col.values())
    start(q_near.values())
    start(k_col.values())
    start(v_row.values())

    q_pos = []
    for i in range(ZQ):
        at_pb, at_kv = line(-RING8[i])
        q_pos.append(jnp.full((1, B), order_ref[at_kv * 32 + at_pb], jnp.int32))
    q_pos = jnp.concatenate(q_pos, axis=1)
    for t in range(4):
        for b in range(4):
            at_pb = z_hi * 16 + ys[-RING4[t] % 4] * 4 + xs[-RING4[b] % 4]
            for r in range(2):
                k_pos = order_ref[(kv + r * (1 - 2 * core)) * 32 + at_pb]
                bias[2 * t + r, b : b + 1, :] = jnp.where(k_pos > q_pos, BIG, 0.0)

    def pair(i, which):
        return jnp.concatenate([qg[2 * i, which], qg[2 * i + 1, which]], axis=1)

    def chunk(t, r, which):
        return kvg[t, r, which].reshape(KC, B)

    def tile(t, r, i, own=False):
        j = 2 * t + r
        at = pl.ds(pl.multiple_of(i * CQ, CQ), CQ)
        s = dot(chunk(t, r, 0), pair(i, 0), 1, 0).reshape(4, B, CQ)
        if own:
            lane = lax.broadcasted_iota(jnp.int32, (B, CQ), 1)
            sub = lax.broadcasted_iota(jnp.int32, (B, CQ), 0)
            later = jnp.where((sub > lane) & (lane < B), -BIG, 0.0)
            s = jnp.concatenate([s[0:1] + later[None], s[1:]], axis=0)
        off = bias[j, :, at] > 0
        rowmax = jnp.max(jnp.where(off, -BIG, jnp.max(s, axis=1)), axis=0, keepdims=True)
        shift = jnp.where(off, BIG, rowmax)
        p = jnp.exp2((s - shift[:, None, :]) * log_scale).reshape(KC, CQ)
        dp = dot(chunk(t, r, 1), pair(i, 1), 1, 0)
        one = pl.ds(j, 1)
        maxes[one, at] = rowmax
        totals[one, at] = jnp.sum(p, axis=0, keepdims=True)
        deltas[one, at] = jnp.sum(p * dp, axis=0, keepdims=True)
        probs[j, :, at] = p.astype(BF16)
        dprobs[j, :, at] = dp

    def loop(start, stop, step):
        def one(i, carry):
            step(i)
            return carry

        lax.fori_loop(start, stop, one, 0)

    def tiles_by_query(t, r, stop):
        loop(0, stop, lambda i: tile(t, r, i))

    def tiles_by_chunk(stop, i):
        loop(0, stop, lambda j: tile(j // 2, lax.rem(j, 2), i))

    def key_row(t):
        arrived([k_col[t], k_on[t]] + v_on[t])
        start([share[t]])

    arrived(k_row.values())
    start(k_on.values())
    arrived(v_col.values())
    for t in (1, 2, 3):
        start(v_on[t])
    arrived([q_near[3], q_near[4]])
    for i in (5, 6, 7):
        start(q_on[i])
    arrived(v_row.values())
    start([share[0]])
    arrived([q_near[1], q_near[2]])
    tile(0, 0, 0, own=True)
    tile(0, 0, 1)
    arrived([share[0]])
    tiles_by_query(0, 1, 2)
    key_row(1)
    tiles_by_query(1, 0, 2)
    key_row(2)
    arrived([share[1]])
    tiles_by_query(1, 1, 2)
    arrived(q_on[5])
    key_row(3)
    tiles_by_chunk(4, 2)
    arrived([share[2]])
    loop(0, 3, lambda i: [tile(2, 0, i), tile(2, 1, i)])
    arrived(q_on[6] + q_on[7])
    tiles_by_chunk(6, 3)
    arrived([share[3]])
    loop(0, 4, lambda i: [tile(3, 0, i), tile(3, 1, i)])

    top = jnp.max(maxes[...], axis=0, keepdims=True)
    factor = jnp.exp2((maxes[...] - top) * log_scale)
    total = jnp.maximum(jnp.sum(factor * totals[...], axis=0, keepdims=True), TINY)
    near = top * log_scale + jnp.log2(total)
    mean = jnp.sum(factor * deltas[...], axis=0, keepdims=True) / total
    factors[...] = factor / total
    for i in range(ZQ):
        one = pl.ds(zs[-RING8[i] % 8], 1)
        st_send[0, one, :] = near[:, i * B : (i + 1) * B]
        st_send[1, one, :] = mean[:, i * B : (i + 1) * B]
    stats = [copy(st_send, st_recv.at[z], line(RING8[i])) for i in range(1, ZQ)]
    start(stats)
    st_recv[z] = st_send[...]

    def turn(j):
        t, r = j // 2, lax.rem(j, 2)
        kt[j] = chunk(t, r, 0).T
        vt[j] = chunk(t, r, 1).T

    loop(0, CHUNKS, turn)

    def attend(i):
        at = pl.ds(pl.multiple_of(i * CQ, CQ), CQ)
        accum = jnp.zeros((B, CQ), F32)
        for j in range(CHUNKS):
            accum += dot(vt[j], probs[j, :, at], 1, 0) * factors[j : j + 1, at]
        accum = accum.astype(BF16)
        o_send[2 * i] = accum[:, :B]
        o_send[2 * i + 1] = accum[:, B:]

    loop(0, ZQ // 2, attend)
    o_copies = [copy(o_send.at[i], o_recv.at[i], line(-RING8[i])) for i in range(1, ZQ)]
    start(o_copies)
    o_recv[0] = o_send[0]

    arrived(stats)
    nears, means = st_recv[:, 0], st_recv[:, 1]
    top = jnp.max(nears, axis=0)
    lse = top + jnp.log2(jnp.sum(jnp.exp2(nears - top[None]), axis=0))
    rows[0:8, :] = lse
    rows[8:16, :] = jnp.sum(jnp.exp2(nears - lse[None]) * means, axis=0)

    def row_of(first):
        return jnp.concatenate([rows[pl.ds(first + zs[-RING8[i] % 8], 1), :] for i in range(ZQ)], axis=1)

    maxes[...] = jnp.exp2(maxes[...] * log_scale - row_of(0))
    deltas[0:1, :] = row_of(8)

    def backward_q(i):
        at = pl.ds(pl.multiple_of(i * CQ, CQ), CQ)
        accum = jnp.zeros((B, CQ), F32)
        for j in range(CHUNKS):
            p = probs[j, :, at].astype(F32) * maxes[j : j + 1, at]
            probs[j, :, at] = p.astype(BF16)
            ds = (p * (dprobs[j, :, at] - deltas[0:1, at])).astype(BF16)
            dscores[j, :, at] = ds
            accum += dot(kt[j], ds, 1, 0)
        accum = (accum * scale).astype(BF16)
        dq_send[2 * i] = accum[:, :B]
        dq_send[2 * i + 1] = accum[:, B:]

    dq_copies = [copy(dq_send.at[i], dq_recv.at[i], line(-RING8[i])) for i in range(1, ZQ)]
    loop(0, ZQ // 2, backward_q)
    start(dq_copies)
    dq_recv[0] = dq_send[0]

    def whole(which):
        return jnp.concatenate([qg[i, which] for i in range(ZQ)], axis=1)

    def key_terms(t, r):
        j = 2 * t + r
        dk = dot(dscores[j], whole(0), 1, 1) * scale
        dv = dot(probs[j], whole(1), 1, 1)
        return dk.reshape(4, B, B), dv.reshape(4, B, B)

    swap = {t: copy(pre_send.at[t], pre_recv.at[t], sibling) for t in range(4)}
    dk_out = {t: copy(dk_row.at[t], dk_got.at[t], column(-RING4[t])) for t in (1, 2, 3)}
    dv_out = {
        t: [copy(dv_col.at[t, b], dv_got.at[t, b], row(-RING4[b])) for b in (1, 2, 3)] for t in range(4)
    }
    dk_end = {b: copy(dk_turn.at[b], dk_last.at[b], row(-RING4[b])) for b in (1, 2, 3)}
    dv_end = {t: copy(dv_turn.at[t], dv_last.at[t], column(-RING4[t])) for t in (1, 2, 3)}

    def key_grads(t):
        dk, dv = key_terms(t, 1)
        pre_send[t, 0] = dk.astype(BF16)
        pre_send[t, 1] = dv.astype(BF16)
        start([swap[t]])
        dk, dv = key_terms(t, 0)
        part[0] = dk
        part[1] = dv
        arrived([swap[t]])
        dk_row[t] = (part[0] + pre_recv[t, 0].astype(F32)).astype(BF16)
        dv_col[t] = (part[1] + pre_recv[t, 1].astype(F32)).astype(BF16)
        if t:
            start([dk_out[t]])
        start(dv_out[t])

    def column_sum(t):
        arrived(dv_out[t])
        whole_sum = dv_col[t, 0].astype(F32)
        for b in (1, 2, 3):
            whole_sum += dv_got[t, b].astype(F32)
        return whole_sum

    def dv_pass(t):
        dv_turn[t] = column_sum(t).astype(BF16)
        start([dv_end[t]])

    key_grads(3)
    key_grads(2)
    key_grads(1)
    dv_pass(3)
    key_grads(0)
    arrived(dk_out.values())
    turned = dk_row[0].astype(F32)
    for t in (1, 2, 3):
        turned += dk_got[t].astype(F32)
    dk_turn[...] = turned.astype(BF16)
    start(dk_end.values())
    dv_pass(2)
    dv_pass(1)

    arrived(o_copies)
    out = jnp.zeros((B, B), F32)
    for i in range(ZQ):
        weight = jnp.exp2(st_recv[zs[RING8[i]], 0, pl.ds(z, 1), :] - rows[pl.ds(z, 1), :])
        out += o_recv[i].astype(F32) * weight
    out_ref[...] = out.astype(BF16).T
    arrived(dq_copies)
    dq_ref[...] = jnp.sum(dq_recv[...].astype(F32), axis=0).astype(BF16).T
    total_v = column_sum(0)
    arrived(dv_end.values())
    for t in (1, 2, 3):
        total_v += dv_last[t].astype(F32)
    dv_ref[...] = total_v.astype(BF16)
    total_k = dk_turn[0].astype(F32)
    arrived(dk_end.values())
    for b in (1, 2, 3):
        total_k += dk_last[b].astype(F32)
    dk_ref[...] = total_k.astype(BF16)
    for one in sent:
        one.wait_send()


def finish(a_ref, b_ref, c_ref, d_ref, *outs):
    for src, dst in zip((a_ref, b_ref, c_ref, d_ref), outs):
        dst[...] = src[...]


def per_device(queries, keys, values, grad_out, block_order):
    vmem = pl.BlockSpec(memory_space=pltpu.VMEM)
    block = jax.ShapeDtypeStruct((B, B), BF16)
    parts = pl.pallas_call(
        kernel,
        out_shape=[block] * 4,
        in_specs=[vmem] * 4 + [pl.BlockSpec(memory_space=pltpu.SMEM)],
        out_specs=[vmem] * 4,
        scratch_shapes=[
            pltpu.VMEM((ZQ, 2, B, B), BF16),
            pltpu.VMEM((4, 2, 2, 4, B, B), BF16),
            pltpu.VMEM((CHUNKS, B, KC), BF16),
            pltpu.VMEM((CHUNKS, B, KC), BF16),
            pltpu.VMEM((CHUNKS, 4, NQ), F32),
            pltpu.VMEM((CHUNKS, NQ), F32),
            pltpu.VMEM((CHUNKS, NQ), F32),
            pltpu.VMEM((CHUNKS, NQ), F32),
            pltpu.VMEM((CHUNKS, NQ), F32),
            pltpu.VMEM((16, B), F32),
            pltpu.VMEM((CHUNKS, KC, NQ), BF16),
            pltpu.VMEM((CHUNKS, KC, NQ), F32),
            pltpu.VMEM((CHUNKS, KC, NQ), BF16),
            pltpu.VMEM((2, 8, B), F32),
            pltpu.VMEM((ZQ, 2, 8, B), F32),
            pltpu.VMEM((ZQ, B, B), BF16),
            pltpu.VMEM((ZQ, B, B), BF16),
            pltpu.VMEM((ZQ, B, B), BF16),
            pltpu.VMEM((ZQ, B, B), BF16),
            pltpu.VMEM((4, 2, 4, B, B), BF16),
            pltpu.VMEM((4, 2, 4, B, B), BF16),
            pltpu.VMEM((2, 4, B, B), F32),
            pltpu.VMEM((4, 4, B, B), BF16),
            pltpu.VMEM((4, 4, B, B), BF16),
            pltpu.VMEM((4, B, B), BF16),
            pltpu.VMEM((4, B, B), BF16),
            pltpu.VMEM((4, 4, B, B), BF16),
            pltpu.VMEM((4, 4, B, B), BF16),
            pltpu.VMEM((4, B, B), BF16),
            pltpu.VMEM((4, B, B), BF16),
            pltpu.SemaphoreType.DMA((SEMS,)),
            pltpu.SemaphoreType.DMA((SEMS,)),
        ],
        compiler_params=pltpu.CompilerParams(
            collective_id=0, has_side_effects=True, vmem_limit_bytes=60 * 2**20
        ),
        name="attention",
    )(queries, keys, values, grad_out, block_order)
    return pl.pallas_call(
        finish, out_shape=[block] * 4, in_specs=[vmem] * 4, out_specs=[vmem] * 4, name="finish"
    )(*parts)


def solution(mesh):
    spec = P(("kv", "pb"), None)
    return jax.shard_map(
        per_device, mesh=mesh, in_specs=(spec, spec, spec, spec, P()), out_specs=(spec,) * 4,
        check_vma=False,
    )
```

```python
import jax
import jax.numpy as jnp
from jax import lax
from jax.experimental import pallas as pl
from jax.experimental.pallas import tpu as pltpu
from jax.sharding import PartitionSpec as P

MESH = pl.DeviceIdType.MESH
F32 = jnp.float32
BF16 = jnp.bfloat16
BIG = 1e30
TINY = 1e-30
B = 128
ZQ = 8
NQ = ZQ * B
CHUNKS = 8
KC = 4 * B
CH = 4 * B
RING4 = (0, 1, 3, 2)
RING8 = (0, 1, 7, 2, 6, 3, 5, 4)


class Sems:
    def __init__(self):
        self.count = 0

    def take(self):
        self.count += 1
        return self.count - 1


SEMS = 82

def dot(left, right, left_dim, right_dim):
    return lax.dot_general(
        left, right, (((left_dim,), (right_dim,)), ((), ())), preferred_element_type=F32
    )


def kernel(
    q_ref, k_ref, v_ref, g_ref, order_ref,
    out_ref, dq_ref, dk_ref, dv_ref,
    qg, kvg, kt, vt, bias, maxes, totals, deltas, factors, rowdelta, rows, probs, dprobs, dscores,
    st_send, st_recv, o_send, o_recv, dq_send, dq_recv, pre_send, pre_recv, part,
    dk_row, dk_got, dk_turn, dk_last, dv_col, dv_got, dv_turn, dv_last,
    ssem, rsem,
):
    scale = B ** -0.5
    log_scale = scale * 1.4426950408889634
    pb, kv = lax.axis_index("pb"), lax.axis_index("kv")
    place = lax.rem(pb, 16)
    x, y = lax.rem(place, 4), place // 4
    z_hi = pb // 16
    z, core = z_hi * 4 + kv // 2, lax.rem(kv, 2)

    xs = [lax.rem(x + d, 4) for d in range(4)]
    ys = [lax.rem(y + d, 4) for d in range(4)]
    zs = [lax.rem(z + d, 8) for d in range(8)]
    pb_z = [at // 4 * 16 + place for at in zs]
    kv_z = [lax.rem(at, 4) * 2 + core for at in zs]

    def row(dx):
        return (z_hi * 16 + y * 4 + xs[dx % 4], kv)

    def column(dy):
        return (z_hi * 16 + ys[dy % 4] * 4 + x, kv)

    def line(dz):
        return (pb_z[dz % 8], kv_z[dz % 8])

    sibling = (pb, kv + 1 - 2 * core)
    sems = Sems()

    def copy(src, dst, peer):
        at = sems.take()
        return pltpu.make_async_remote_copy(
            src_ref=src, dst_ref=dst, send_sem=ssem.at[at], recv_sem=rsem.at[at],
            device_id=peer, device_id_type=MESH,
        )

    sent = []

    def start(copies):
        for one in copies:
            one.start()
            sent.append(one)

    def arrived(copies):
        for one in copies:
            one.wait_recv()

    barrier = pltpu.get_barrier_semaphore()
    peers = [line(d) for d in range(1, 8)] + [f(d) for f in (row, column) for d in (1, 2, 3)] + [sibling]
    for peer in peers:
        pl.semaphore_signal(barrier, inc=1, device_id=peer, device_id_type=MESH)
    qg[0, 0] = q_ref[...].T
    qg[0, 1] = g_ref[...].T
    kvg[0, 0, 0, 0] = k_ref[...]
    kvg[0, 0, 1, 0] = v_ref[...]
    pl.semaphore_wait(barrier, len(peers))

    k_row = {b: copy(kvg.at[0, 0, 0, 0], kvg.at[0, 0, 0, b], row(RING4[b])) for b in (1, 2, 3)}
    v_col = {t: copy(kvg.at[0, 0, 1, 0], kvg.at[t, 0, 1, 0], column(RING4[t])) for t in (1, 2, 3)}
    q_near = {i: copy(qg.at[0], qg.at[i], line(RING8[i])) for i in (3, 4, 1, 2)}
    k_col = {t: copy(kvg.at[0, 0, 0, 0], kvg.at[t, 0, 0, 0], column(RING4[t])) for t in (1, 2, 3)}
    v_row = {b: copy(kvg.at[0, 0, 1, 0], kvg.at[0, 0, 1, b], row(RING4[b])) for b in (1, 2, 3)}
    k_on = {t: copy(kvg.at[0, 0, 0, pl.ds(1, 3)], kvg.at[t, 0, 0, pl.ds(1, 3)], column(RING4[t])) for t in (1, 2, 3)}
    v_on = {
        t: [copy(kvg.at[t, 0, 1, 0], kvg.at[t, 0, 1, b], row(RING4[b])) for b in (1, 2, 3)] for t in (1, 2, 3)
    }
    q_on = {
        5: [copy(qg.at[3], qg.at[5], line(1))],
        6: [copy(qg.at[4], qg.at[6], line(-1))],
        7: [copy(qg.at[3, 0], qg.at[7, 0], line(2)), copy(qg.at[4, 1], qg.at[7, 1], line(-2))],
    }
    share = [copy(kvg.at[t, 0], kvg.at[t, 1], sibling) for t in range(4)]

    start(k_row.values())
    start(v_col.values())
    start(q_near.values())
    start(k_col.values())
    start(v_row.values())

    q_pos = []
    for i in range(ZQ):
        at_pb, at_kv = line(-RING8[i])
        q_pos.append(jnp.full((1, B), order_ref[at_kv * 32 + at_pb], jnp.int32))
    q_pos = jnp.concatenate(q_pos, axis=1)
    for t in range(4):
        for b in range(4):
            at_pb = z_hi * 16 + ys[-RING4[t] % 4] * 4 + xs[-RING4[b] % 4]
            for r in range(2):
                k_pos = order_ref[(kv + r * (1 - 2 * core)) * 32 + at_pb]
                bias[2 * t + r, b : b + 1, :] = jnp.where(k_pos > q_pos, BIG, 0.0)

    def quad(half, which):
        return jnp.concatenate([qg[4 * half + i, which] for i in range(4)], axis=1)

    def chunk(t, r, which):
        return kvg[t, r, which].reshape(KC, B)

    def unit(t, r, half, own=False):
        j = 2 * t + r
        at = slice(half * CH, (half + 1) * CH)
        s = dot(chunk(t, r, 0), quad(half, 0), 1, 0)
        dp = dot(chunk(t, r, 1), quad(half, 1), 1, 0)
        for b in range(4):
            here = slice(b * B, (b + 1) * B)
            sb, db = s[here], dp[here]
            if own and b == 0:
                lane = lax.broadcasted_iota(jnp.int32, (B, B), 1)
                sub = lax.broadcasted_iota(jnp.int32, (B, B), 0)
                first = sb[:, :B] + jnp.where(sub > lane, -BIG, 0.0)
                sb = jnp.concatenate([first, sb[:, B:]], axis=1)
            top = jnp.max(sb, axis=0, keepdims=True)
            p = jnp.exp2((sb - top) * log_scale)
            maxes[j, b : b + 1, at] = top
            totals[j, b : b + 1, at] = jnp.sum(p, axis=0, keepdims=True)
            deltas[j, b : b + 1, at] = jnp.sum(p * db, axis=0, keepdims=True)
            probs[j, here, at] = p.astype(BF16)
        dprobs[j, :, at] = dp

    def loop(start, stop, step):
        def one(i, carry):
            step(i)
            return carry

        lax.fori_loop(start, stop, one, 0)

    def key_row(t):
        arrived([k_col[t], k_on[t]] + v_on[t])
        start([share[t]])

    arrived(k_row.values())
    start(k_on.values())
    arrived(v_col.values())
    for t in (1, 2, 3):
        start(v_on[t])
    arrived([q_near[3], q_near[4]])
    for i in (5, 6, 7):
        start(q_on[i])
    arrived(v_row.values())
    start([share[0]])
    arrived([q_near[1], q_near[2]])
    unit(0, 0, 0, own=True)
    for t in (1, 2, 3):
        key_row(t)
        arrived([share[t - 1]])
        unit(t - 1, 1, 0)
        unit(t, 0, 0)
    arrived(q_on[5] + q_on[6] + q_on[7])
    loop(0, 3, lambda t: [unit(t, 0, 1), unit(t, 1, 1)])
    arrived([share[3]])
    unit(3, 0, 1)
    unit(3, 1, 1)
    unit(3, 1, 0)
    off = bias[...] > 0
    top = jnp.max(jnp.where(off, -BIG, maxes[...]), axis=(0, 1), keepdims=True)
    factor = jnp.where(off, 0.0, jnp.exp2((maxes[...] - top) * log_scale))
    total = jnp.maximum(jnp.sum(factor * totals[...], axis=(0, 1), keepdims=True), TINY)
    near = (top * log_scale + jnp.log2(total))[0]
    mean = (jnp.sum(factor * deltas[...], axis=(0, 1), keepdims=True) / total)[0]
    factors[...] = factor / total
    for i in range(ZQ):
        one = pl.ds(zs[-RING8[i] % 8], 1)
        st_send[0, one, :] = near[:, i * B : (i + 1) * B]
        st_send[1, one, :] = mean[:, i * B : (i + 1) * B]
    stats = [copy(st_send, st_recv.at[z], line(RING8[i])) for i in range(1, ZQ)]
    start(stats)
    st_recv[z] = st_send[...]

    def turn(j):
        t, r = j // 2, lax.rem(j, 2)
        kt[j] = chunk(t, r, 0).T
        vt[j] = chunk(t, r, 1).T

    loop(0, CHUNKS, turn)

    def scaled(j, at):
        p = probs[j, :, at].astype(F32).reshape(4, B, CH) * factors[j, :, at][:, None, :]
        return p.reshape(KC, CH)

    def attend(half):
        at = pl.ds(pl.multiple_of(half * CH, CH), CH)
        accum = jnp.zeros((B, CH), F32)
        for j in range(CHUNKS):
            accum += dot(vt[j], scaled(j, at).astype(BF16), 1, 0)
        accum = accum.astype(BF16)
        for i in range(4):
            o_send[4 * half + i] = accum[:, i * B : (i + 1) * B]

    loop(0, 2, attend)
    o_copies = [copy(o_send.at[i], o_recv.at[i], line(-RING8[i])) for i in range(1, ZQ)]
    start(o_copies)
    o_recv[0] = o_send[0]

    arrived(stats)
    nears, means = st_recv[:, 0], st_recv[:, 1]
    top = jnp.max(nears, axis=0)
    lse = top + jnp.log2(jnp.sum(jnp.exp2(nears - top[None]), axis=0))
    rows[0:8, :] = lse
    rows[8:16, :] = jnp.sum(jnp.exp2(nears - lse[None]) * means, axis=0)

    def row_of(first):
        return jnp.concatenate([rows[pl.ds(first + zs[-RING8[i] % 8], 1), :] for i in range(ZQ)], axis=1)

    factors[...] = jnp.where(off, 0.0, jnp.exp2(maxes[...] * log_scale - row_of(0)[None]))
    rowdelta[...] = row_of(8)

    dq_copies = {i: copy(dq_send.at[i], dq_recv.at[i], line(-RING8[i])) for i in range(1, ZQ)}

    def backward_q(half):
        at = slice(half * CH, (half + 1) * CH)
        accum = jnp.zeros((B, CH), F32)
        for j in range(CHUNKS):
            p = scaled(j, at)
            probs[j, :, at] = p.astype(BF16)
            ds = (p * (dprobs[j, :, at] - rowdelta[:, at])).astype(BF16)
            dscores[j, :, at] = ds
            accum += dot(kt[j], ds, 1, 0)
        accum = (accum * scale).astype(BF16)
        for i in range(4 * half, 4 * half + 4):
            dq_send[i] = accum[:, (i - 4 * half) * B : (i - 4 * half + 1) * B]
        start([dq_copies[i] for i in range(4 * half + 3, 4 * half - 1, -1) if i])

    backward_q(1)
    backward_q(0)
    dq_recv[0] = dq_send[0]

    def whole(which):
        return jnp.concatenate([qg[i, which] for i in range(ZQ)], axis=1)

    def key_terms(t, r):
        j = 2 * t + r
        dk = dot(dscores[j], whole(0), 1, 1) * scale
        dv = dot(probs[j], whole(1), 1, 1)
        return dk.reshape(4, B, B), dv.reshape(4, B, B)

    swap = {t: copy(pre_send.at[t], pre_recv.at[t], sibling) for t in range(4)}
    dk_out = {t: copy(dk_row.at[t], dk_got.at[t], column(-RING4[t])) for t in (1, 2, 3)}
    dv_out = {
        t: [copy(dv_col.at[t, b], dv_got.at[t, b], row(-RING4[b])) for b in (1, 2, 3)] for t in range(4)
    }
    dk_end = {b: copy(dk_turn.at[b], dk_last.at[b], row(-RING4[b])) for b in (1, 2, 3)}
    dv_end = {t: copy(dv_turn.at[t], dv_last.at[t], column(-RING4[t])) for t in (1, 2, 3)}

    def send_half(t):
        dk, dv = key_terms(t, 1)
        pre_send[t, 0] = dk.astype(BF16)
        pre_send[t, 1] = dv.astype(BF16)
        start([swap[t]])

    def keep_half(t):
        dk, dv = key_terms(t, 0)
        part[0] = dk
        part[1] = dv
        arrived([swap[t]])
        dk_row[t] = (part[0] + pre_recv[t, 0].astype(F32)).astype(BF16)
        dv_col[t] = (part[1] + pre_recv[t, 1].astype(F32)).astype(BF16)
        if t:
            start([dk_out[t]])
        start(dv_out[t])

    def column_sum(t):
        arrived(dv_out[t])
        whole_sum = dv_col[t, 0].astype(F32)
        for b in (1, 2, 3):
            whole_sum += dv_got[t, b].astype(F32)
        return whole_sum

    def dv_pass(t):
        dv_turn[t] = column_sum(t).astype(BF16)
        start([dv_end[t]])

    send_half(3)
    send_half(2)
    keep_half(3)
    send_half(1)
    keep_half(2)
    send_half(0)
    keep_half(1)
    dv_pass(3)
    keep_half(0)
    arrived(dk_out.values())
    turned = dk_row[0].astype(F32)
    for t in (1, 2, 3):
        turned += dk_got[t].astype(F32)
    dk_turn[...] = turned.astype(BF16)
    start(dk_end.values())
    dv_pass(2)
    dv_pass(1)

    arrived(o_copies)
    out = jnp.zeros((B, B), F32)
    for i in range(ZQ):
        weight = jnp.exp2(st_recv[zs[RING8[i]], 0, pl.ds(z, 1), :] - rows[pl.ds(z, 1), :])
        out += o_recv[i].astype(F32) * weight
    out_ref[...] = out.astype(BF16).T
    arrived(dq_copies.values())
    dq_ref[...] = jnp.sum(dq_recv[...].astype(F32), axis=0).astype(BF16).T
    total_v = column_sum(0)
    arrived(dv_end.values())
    for t in (1, 2, 3):
        total_v += dv_last[t].astype(F32)
    dv_ref[...] = total_v.astype(BF16)
    total_k = dk_turn[0].astype(F32)
    arrived(dk_end.values())
    for b in (1, 2, 3):
        total_k += dk_last[b].astype(F32)
    dk_ref[...] = total_k.astype(BF16)
    for one in sent:
        one.wait_send()


def finish(a_ref, b_ref, c_ref, d_ref, *outs):
    for src, dst in zip((a_ref, b_ref, c_ref, d_ref), outs):
        dst[...] = src[...]


def per_device(queries, keys, values, grad_out, block_order):
    vmem = pl.BlockSpec(memory_space=pltpu.VMEM)
    block = jax.ShapeDtypeStruct((B, B), BF16)
    parts = pl.pallas_call(
        kernel,
        out_shape=[block] * 4,
        in_specs=[vmem] * 4 + [pl.BlockSpec(memory_space=pltpu.SMEM)],
        out_specs=[vmem] * 4,
        scratch_shapes=[
            pltpu.VMEM((ZQ, 2, B, B), BF16),
            pltpu.VMEM((4, 2, 2, 4, B, B), BF16),
            pltpu.VMEM((CHUNKS, B, KC), BF16),
            pltpu.VMEM((CHUNKS, B, KC), BF16),
            pltpu.VMEM((CHUNKS, 4, NQ), F32),
            pltpu.VMEM((CHUNKS, 4, NQ), F32),
            pltpu.VMEM((CHUNKS, 4, NQ), F32),
            pltpu.VMEM((CHUNKS, 4, NQ), F32),
            pltpu.VMEM((CHUNKS, 4, NQ), F32),
            pltpu.VMEM((1, NQ), F32),
            pltpu.VMEM((16, B), F32),
            pltpu.VMEM((CHUNKS, KC, NQ), BF16),
            pltpu.VMEM((CHUNKS, KC, NQ), F32),
            pltpu.VMEM((CHUNKS, KC, NQ), BF16),
            pltpu.VMEM((2, 8, B), F32),
            pltpu.VMEM((ZQ, 2, 8, B), F32),
            pltpu.VMEM((ZQ, B, B), BF16),
            pltpu.VMEM((ZQ, B, B), BF16),
            pltpu.VMEM((ZQ, B, B), BF16),
            pltpu.VMEM((ZQ, B, B), BF16),
            pltpu.VMEM((4, 2, 4, B, B), BF16),
            pltpu.VMEM((4, 2, 4, B, B), BF16),
            pltpu.VMEM((2, 4, B, B), F32),
            pltpu.VMEM((4, 4, B, B), BF16),
            pltpu.VMEM((4, 4, B, B), BF16),
            pltpu.VMEM((4, B, B), BF16),
            pltpu.VMEM((4, B, B), BF16),
            pltpu.VMEM((4, 4, B, B), BF16),
            pltpu.VMEM((4, 4, B, B), BF16),
            pltpu.VMEM((4, B, B), BF16),
            pltpu.VMEM((4, B, B), BF16),
            pltpu.SemaphoreType.DMA((SEMS,)),
            pltpu.SemaphoreType.DMA((SEMS,)),
        ],
        compiler_params=pltpu.CompilerParams(
            collective_id=0, has_side_effects=True, vmem_limit_bytes=60 * 2**20
        ),
        name="attention",
    )(queries, keys, values, grad_out, block_order)
    return pl.pallas_call(
        finish, out_shape=[block] * 4, in_specs=[vmem] * 4, out_specs=[vmem] * 4, name="finish"
    )(*parts)


def solution(mesh):
    spec = P(("kv", "pb"), None)
    return jax.shard_map(
        per_device, mesh=mesh, in_specs=(spec, spec, spec, spec, P()), out_specs=(spec,) * 4,
        check_vma=False,
    )
```

```python
import jax
import jax.numpy as jnp
from jax import lax
from jax.experimental import pallas as pl
from jax.experimental.pallas import tpu as pltpu
from jax.sharding import PartitionSpec as P

MESH = pl.DeviceIdType.MESH
F32 = jnp.float32
BF16 = jnp.bfloat16
BIG = 1e30
TINY = 1e-30
B = 128
ZQ = 8
NQ = ZQ * B
CHUNKS = 8
KC = 4 * B
CH = 4 * B
RING4 = (0, 1, 3, 2)
RING8 = (0, 1, 7, 2, 6, 3, 5, 4)


class Sems:
    def __init__(self):
        self.count = 0

    def take(self):
        self.count += 1
        return self.count - 1


SEMS = 82

def dot(left, right, left_dim, right_dim):
    return lax.dot_general(
        left, right, (((left_dim,), (right_dim,)), ((), ())), preferred_element_type=F32
    )


def kernel(
    q_ref, k_ref, v_ref, g_ref, order_ref,
    out_ref, dq_ref, dk_ref, dv_ref,
    qg, kvg, kt, vt, bias, maxes, totals, deltas, factors, rowdelta, rows, probs, dprobs, dscores,
    st_send, st_recv, o_send, o_recv, dq_send, dq_recv, pre_send, pre_recv, part,
    dk_row, dk_got, dk_turn, dk_last, dv_col, dv_got, dv_turn, dv_last,
    ssem, rsem,
):
    scale = B ** -0.5
    log_scale = scale * 1.4426950408889634
    pb, kv = lax.axis_index("pb"), lax.axis_index("kv")
    place = lax.rem(pb, 16)
    x, y = lax.rem(place, 4), place // 4
    z_hi = pb // 16
    z, core = z_hi * 4 + kv // 2, lax.rem(kv, 2)

    xs = [lax.rem(x + d, 4) for d in range(4)]
    ys = [lax.rem(y + d, 4) for d in range(4)]
    zs = [lax.rem(z + d, 8) for d in range(8)]
    pb_z = [at // 4 * 16 + place for at in zs]
    kv_z = [lax.rem(at, 4) * 2 + core for at in zs]

    def row(dx):
        return (z_hi * 16 + y * 4 + xs[dx % 4], kv)

    def column(dy):
        return (z_hi * 16 + ys[dy % 4] * 4 + x, kv)

    def line(dz):
        return (pb_z[dz % 8], kv_z[dz % 8])

    sibling = (pb, kv + 1 - 2 * core)
    sems = Sems()

    def copy(src, dst, peer):
        at = sems.take()
        return pltpu.make_async_remote_copy(
            src_ref=src, dst_ref=dst, send_sem=ssem.at[at], recv_sem=rsem.at[at],
            device_id=peer, device_id_type=MESH,
        )

    sent = []

    def start(copies):
        for one in copies:
            one.start()
            sent.append(one)

    def left():
        for one in sent:
            one.wait_send()
        sent.clear()

    def arrived(copies):
        for one in copies:
            one.wait_recv()

    barrier = pltpu.get_barrier_semaphore()
    peers = [line(d) for d in range(1, 8)] + [f(d) for f in (row, column) for d in (1, 2, 3)] + [sibling]
    for peer in peers:
        pl.semaphore_signal(barrier, inc=1, device_id=peer, device_id_type=MESH)
    qg[0, 0] = q_ref[...].T
    qg[0, 1] = g_ref[...].T
    kvg[0, 0, 0, 0] = k_ref[...]
    kvg[0, 0, 1, 0] = v_ref[...]
    pl.semaphore_wait(barrier, len(peers))

    k_row = {b: copy(kvg.at[0, 0, 0, 0], kvg.at[0, 0, 0, b], row(RING4[b])) for b in (1, 2, 3)}
    v_col = {t: copy(kvg.at[0, 0, 1, 0], kvg.at[t, 0, 1, 0], column(RING4[t])) for t in (1, 2, 3)}
    q_near = {i: copy(qg.at[0], qg.at[i], line(RING8[i])) for i in (3, 4, 1, 2)}
    k_col = {t: copy(kvg.at[0, 0, 0, 0], kvg.at[t, 0, 0, 0], column(RING4[t])) for t in (1, 2, 3)}
    v_row = {b: copy(kvg.at[0, 0, 1, 0], kvg.at[0, 0, 1, b], row(RING4[b])) for b in (1, 2, 3)}
    k_on = {t: copy(kvg.at[0, 0, 0, pl.ds(1, 3)], kvg.at[t, 0, 0, pl.ds(1, 3)], column(RING4[t])) for t in (1, 2, 3)}
    v_on = {
        t: [copy(kvg.at[t, 0, 1, 0], kvg.at[t, 0, 1, b], row(RING4[b])) for b in (1, 2, 3)] for t in (1, 2, 3)
    }
    q_on = {
        5: [copy(qg.at[3], qg.at[5], line(1))],
        6: [copy(qg.at[4], qg.at[6], line(-1))],
        7: [copy(qg.at[3, 0], qg.at[7, 0], line(2)), copy(qg.at[4, 1], qg.at[7, 1], line(-2))],
    }
    share = [copy(kvg.at[t, 0], kvg.at[t, 1], sibling) for t in range(4)]

    start(k_row.values())
    start(v_col.values())
    start(q_near.values())
    start(k_col.values())
    start(v_row.values())

    q_pos = []
    for i in range(ZQ):
        at_pb, at_kv = line(-RING8[i])
        q_pos.append(jnp.full((1, B), order_ref[at_kv * 32 + at_pb], jnp.int32))
    q_pos = jnp.concatenate(q_pos, axis=1)
    for t in range(4):
        for b in range(4):
            at_pb = z_hi * 16 + ys[-RING4[t] % 4] * 4 + xs[-RING4[b] % 4]
            for r in range(2):
                k_pos = order_ref[(kv + r * (1 - 2 * core)) * 32 + at_pb]
                bias[2 * t + r, b : b + 1, :] = jnp.where(k_pos > q_pos, BIG, 0.0)

    def quad(half, which):
        return jnp.concatenate([qg[4 * half + i, which] for i in range(4)], axis=1)

    def chunk(t, r, which):
        return kvg[t, r, which].reshape(KC, B)

    def unit(t, r, half, own=False):
        j = 2 * t + r
        at = slice(half * CH, (half + 1) * CH)
        s = dot(chunk(t, r, 0), quad(half, 0), 1, 0)
        dp = dot(chunk(t, r, 1), quad(half, 1), 1, 0)
        for b in range(4):
            here = slice(b * B, (b + 1) * B)
            sb, db = s[here], dp[here]
            if own and b == 0:
                lane = lax.broadcasted_iota(jnp.int32, (B, B), 1)
                sub = lax.broadcasted_iota(jnp.int32, (B, B), 0)
                first = sb[:, :B] + jnp.where(sub > lane, -BIG, 0.0)
                sb = jnp.concatenate([first, sb[:, B:]], axis=1)
            top = jnp.max(sb, axis=0, keepdims=True)
            p = jnp.exp2((sb - top) * log_scale)
            maxes[j, b : b + 1, at] = top
            totals[j, b : b + 1, at] = jnp.sum(p, axis=0, keepdims=True)
            deltas[j, b : b + 1, at] = jnp.sum(p * db, axis=0, keepdims=True)
            probs[j, here, at] = p.astype(BF16)
        dprobs[j, :, at] = dp

    def key_row(t):
        arrived([k_col[t], k_on[t]] + v_on[t])
        start([share[t]])

    arrived(k_row.values())
    start(k_on.values())
    arrived(v_col.values())
    for t in (1, 2, 3):
        start(v_on[t])
    arrived([q_near[3], q_near[4]])
    for i in (5, 6, 7):
        start(q_on[i])
    arrived(v_row.values())
    start([share[0]])
    arrived([q_near[1], q_near[2]])
    unit(0, 0, 0, own=True)
    for t in (1, 2, 3):
        key_row(t)
        unit(t, 0, 0)
    arrived([share[0], share[1]])
    unit(0, 1, 0)
    unit(1, 1, 0)
    arrived(q_on[5] + q_on[6] + q_on[7])
    for t in range(4):
        unit(t, 0, 1)
    unit(0, 1, 1)
    unit(1, 1, 1)
    arrived([share[2], share[3]])
    for t in (2, 3):
        unit(t, 1, 0)
        unit(t, 1, 1)
    off = bias[...] > 0
    top = jnp.max(jnp.where(off, -BIG, maxes[...]), axis=(0, 1), keepdims=True)
    factor = jnp.where(off, 0.0, jnp.exp2((maxes[...] - top) * log_scale))
    total = jnp.maximum(jnp.sum(factor * totals[...], axis=(0, 1), keepdims=True), TINY)
    near = (top * log_scale + jnp.log2(total))[0]
    mean = (jnp.sum(factor * deltas[...], axis=(0, 1), keepdims=True) / total)[0]
    factors[...] = factor / total
    for i in range(ZQ):
        one = pl.ds(zs[-RING8[i] % 8], 1)
        st_send[0, one, :] = near[:, i * B : (i + 1) * B]
        st_send[1, one, :] = mean[:, i * B : (i + 1) * B]
    stats = [copy(st_send, st_recv.at[z], line(RING8[i])) for i in range(1, ZQ)]
    gathered = list(sent)
    sent.clear()
    start(stats)
    st_recv[z] = st_send[...]

    def turn(j):
        t, r = j // 2, j % 2
        kt[j] = chunk(t, r, 0).T
        vt[j] = chunk(t, r, 1).T

    for j in range(CHUNKS):
        turn(j)

    def scaled(j, at):
        p = probs[j, :, at].astype(F32).reshape(4, B, CH) * factors[j, :, at][:, None, :]
        return p.reshape(KC, CH)

    def attend(half):
        at = slice(half * CH, (half + 1) * CH)
        accum = jnp.zeros((B, CH), F32)
        for j in range(CHUNKS):
            accum += dot(vt[j], scaled(j, at).astype(BF16), 1, 0)
        accum = accum.astype(BF16)
        for i in range(4):
            o_send[4 * half + i] = accum[:, i * B : (i + 1) * B]

    attend(1)
    attend(0)
    o_copies = [copy(o_send.at[i], o_recv.at[i], line(-RING8[i])) for i in range(1, ZQ)]
    start(o_copies)
    o_recv[0] = o_send[0]

    for one in gathered:
        one.wait_send()
    arrived(stats)
    nears, means = st_recv[:, 0], st_recv[:, 1]
    top = jnp.max(nears, axis=0)
    lse = top + jnp.log2(jnp.sum(jnp.exp2(nears - top[None]), axis=0))
    rows[0:8, :] = lse
    rows[8:16, :] = jnp.sum(jnp.exp2(nears - lse[None]) * means, axis=0)

    def row_of(first):
        return jnp.concatenate([rows[pl.ds(first + zs[-RING8[i] % 8], 1), :] for i in range(ZQ)], axis=1)

    factors[...] = jnp.where(off, 0.0, jnp.exp2(maxes[...] * log_scale - row_of(0)[None]))
    rowdelta[...] = row_of(8)

    dq_copies = {i: copy(dq_send.at[i], dq_recv.at[i], line(-RING8[i])) for i in range(1, ZQ)}

    def weigh(j):
        for half in range(2):
            at = slice(half * CH, (half + 1) * CH)
            p = scaled(j, at)
            probs[j, :, at] = p.astype(BF16)
            dscores[j, :, at] = (p * (dprobs[j, :, at] - rowdelta[:, at])).astype(BF16)

    def query_grads(half):
        at = slice(half * CH, (half + 1) * CH)
        accum = jnp.zeros((B, CH), F32)
        for j in range(CHUNKS):
            accum += dot(kt[j], dscores[j, :, at], 1, 0)
        accum = (accum * scale).astype(BF16)
        for i in range(4 * half, 4 * half + 4):
            dq_send[i] = accum[:, (i - 4 * half) * B : (i - 4 * half + 1) * B]
        start([dq_copies[i] for i in range(4 * half + 3, 4 * half - 1, -1) if i])

    def whole(which):
        return jnp.concatenate([qg[i, which] for i in range(ZQ)], axis=1)

    def key_terms(t, r):
        j = 2 * t + r
        dk = dot(dscores[j], whole(0), 1, 1) * scale
        dv = dot(probs[j], whole(1), 1, 1)
        return dk.reshape(4, B, B), dv.reshape(4, B, B)

    swap = {t: copy(pre_send.at[t], pre_recv.at[t], sibling) for t in range(4)}
    dk_out = {t: copy(dk_row.at[t], dk_got.at[t], column(-RING4[t])) for t in (1, 2, 3)}
    dv_out = {
        t: [copy(dv_col.at[t, b], dv_got.at[t, b], row(-RING4[b])) for b in (1, 2, 3)] for t in range(4)
    }
    dk_end = {b: copy(dk_turn.at[b], dk_last.at[b], row(-RING4[b])) for b in (1, 2, 3)}
    dv_end = {t: copy(dv_turn.at[t], dv_last.at[t], column(-RING4[t])) for t in (1, 2, 3)}

    def send_half(t, *following):
        dk, dv = key_terms(t, 1)
        for j in following:
            weigh(j)
        pre_send[t, 0] = dk.astype(BF16)
        pre_send[t, 1] = dv.astype(BF16)
        start([swap[t]])

    def keep_half(t, *following):
        dk, dv = key_terms(t, 0)
        for j in following:
            weigh(j)
        part[t, 0] = dk
        part[t, 1] = dv

    def merge(t):
        arrived([swap[t]])
        dk_row[t] = (part[t, 0] + pre_recv[t, 0].astype(F32)).astype(BF16)
        dv_col[t] = (part[t, 1] + pre_recv[t, 1].astype(F32)).astype(BF16)
        if t:
            start([dk_out[t]])
        start(dv_out[t])

    def column_sum(t):
        arrived(dv_out[t])
        whole_sum = dv_col[t, 0].astype(F32)
        for b in (1, 2, 3):
            whole_sum += dv_got[t, b].astype(F32)
        return whole_sum

    def dv_pass(t):
        dv_turn[t] = column_sum(t).astype(BF16)
        start([dv_end[t]])

    weigh(7)
    send_half(3, 6)
    keep_half(3, 5)
    send_half(2, 4, 3, 2)
    merge(3)
    weigh(1)
    weigh(0)
    query_grads(1)
    query_grads(0)
    dq_recv[0] = dq_send[0]
    keep_half(2)
    merge(2)
    send_half(1)
    send_half(0)
    keep_half(1)
    merge(1)
    keep_half(0)
    merge(0)
    dv_pass(3)
    dv_pass(2)
    dv_pass(1)
    arrived(dk_out.values())
    turned = dk_row[0].astype(F32)
    for t in (1, 2, 3):
        turned += dk_got[t].astype(F32)
    dk_turn[...] = turned.astype(BF16)
    start(dk_end.values())
    arrived(o_copies)
    out = jnp.zeros((B, B), F32)
    for i in range(ZQ):
        weight = jnp.exp2(st_recv[zs[RING8[i]], 0, pl.ds(z, 1), :] - rows[pl.ds(z, 1), :])
        out += o_recv[i].astype(F32) * weight
    out_ref[...] = out.astype(BF16).T
    arrived(dq_copies.values())
    dq_ref[...] = jnp.sum(dq_recv[...].astype(F32), axis=0).astype(BF16).T
    left()
    total_v = column_sum(0)
    arrived(dv_end.values())
    for t in (1, 2, 3):
        total_v += dv_last[t].astype(F32)
    dv_ref[...] = total_v.astype(BF16)
    total_k = dk_turn[0].astype(F32)
    arrived(dk_end.values())
    for b in (1, 2, 3):
        total_k += dk_last[b].astype(F32)
    dk_ref[...] = total_k.astype(BF16)


def finish(a_ref, b_ref, c_ref, d_ref, *outs):
    for src, dst in zip((a_ref, b_ref, c_ref, d_ref), outs):
        dst[...] = src[...]


def per_device(queries, keys, values, grad_out, block_order):
    vmem = pl.BlockSpec(memory_space=pltpu.VMEM)
    block = jax.ShapeDtypeStruct((B, B), BF16)
    parts = pl.pallas_call(
        kernel,
        out_shape=[block] * 4,
        in_specs=[vmem] * 4 + [pl.BlockSpec(memory_space=pltpu.SMEM)],
        out_specs=[vmem] * 4,
        scratch_shapes=[
            pltpu.VMEM((ZQ, 2, B, B), BF16),
            pltpu.VMEM((4, 2, 2, 4, B, B), BF16),
            pltpu.VMEM((CHUNKS, B, KC), BF16),
            pltpu.VMEM((CHUNKS, B, KC), BF16),
            pltpu.VMEM((CHUNKS, 4, NQ), F32),
            pltpu.VMEM((CHUNKS, 4, NQ), F32),
            pltpu.VMEM((CHUNKS, 4, NQ), F32),
            pltpu.VMEM((CHUNKS, 4, NQ), F32),
            pltpu.VMEM((CHUNKS, 4, NQ), F32),
            pltpu.VMEM((1, NQ), F32),
            pltpu.VMEM((16, B), F32),
            pltpu.VMEM((CHUNKS, KC, NQ), BF16),
            pltpu.VMEM((CHUNKS, KC, NQ), F32),
            pltpu.VMEM((CHUNKS, KC, NQ), BF16),
            pltpu.VMEM((2, 8, B), F32),
            pltpu.VMEM((ZQ, 2, 8, B), F32),
            pltpu.VMEM((ZQ, B, B), BF16),
            pltpu.VMEM((ZQ, B, B), BF16),
            pltpu.VMEM((ZQ, B, B), BF16),
            pltpu.VMEM((ZQ, B, B), BF16),
            pltpu.VMEM((4, 2, 4, B, B), BF16),
            pltpu.VMEM((4, 2, 4, B, B), BF16),
            pltpu.VMEM((4, 2, 4, B, B), F32),
            pltpu.VMEM((4, 4, B, B), BF16),
            pltpu.VMEM((4, 4, B, B), BF16),
            pltpu.VMEM((4, B, B), BF16),
            pltpu.VMEM((4, B, B), BF16),
            pltpu.VMEM((4, 4, B, B), BF16),
            pltpu.VMEM((4, 4, B, B), BF16),
            pltpu.VMEM((4, B, B), BF16),
            pltpu.VMEM((4, B, B), BF16),
            pltpu.SemaphoreType.DMA((SEMS,)),
            pltpu.SemaphoreType.DMA((SEMS,)),
        ],
        compiler_params=pltpu.CompilerParams(
            collective_id=0, has_side_effects=True, vmem_limit_bytes=60 * 2**20
        ),
        name="attention",
    )(queries, keys, values, grad_out, block_order)
    return pl.pallas_call(
        finish, out_shape=[block] * 4, in_specs=[vmem] * 4, out_specs=[vmem] * 4, name="finish"
    )(*parts)


def solution(mesh):
    spec = P(("kv", "pb"), None)
    return jax.shard_map(
        per_device, mesh=mesh, in_specs=(spec, spec, spec, spec, P()), out_specs=(spec,) * 4,
        check_vma=False,
    )
```

```python
import jax
import jax.numpy as jnp
from jax import lax
from jax.experimental import pallas as pl
from jax.experimental.pallas import tpu as pltpu
from jax.sharding import PartitionSpec as P

MESH = pl.DeviceIdType.MESH
F32 = jnp.float32
BF16 = jnp.bfloat16
BIG = 1e30
TINY = 1e-30
B = 128
ZQ = 8
NQ = ZQ * B
CHUNKS = 8
KC = 4 * B
CH = 4 * B
RING4 = (0, 1, 3, 2)
RING8 = (0, 1, 7, 2, 6, 3, 5, 4)


class Sems:
    def __init__(self):
        self.count = 0

    def take(self):
        self.count += 1
        return self.count - 1


SEMS = 82

def dot(left, right, left_dim, right_dim):
    return lax.dot_general(
        left, right, (((left_dim,), (right_dim,)), ((), ())), preferred_element_type=F32
    )


def kernel(
    q_ref, k_ref, v_ref, g_ref, order_ref,
    out_ref, dq_ref, dk_ref, dv_ref,
    qg, kvg, kt, vt, bias, maxes, totals, deltas, factors, rowdelta, rows, probs, dprobs, dscores,
    st_send, st_recv, o_send, o_recv, dq_send, dq_recv, pre_send, pre_recv, part,
    dk_row, dk_got, dk_turn, dk_last, dv_col, dv_got, dv_turn, dv_last,
    ssem, rsem,
):
    scale = B ** -0.5
    log_scale = scale * 1.4426950408889634
    pb, kv = lax.axis_index("pb"), lax.axis_index("kv")
    place = lax.rem(pb, 16)
    x, y = lax.rem(place, 4), place // 4
    z_hi = pb // 16
    z, core = z_hi * 4 + kv // 2, lax.rem(kv, 2)

    xs = [lax.rem(x + d, 4) for d in range(4)]
    ys = [lax.rem(y + d, 4) for d in range(4)]
    zs = [lax.rem(z + d, 8) for d in range(8)]
    pb_z = [at // 4 * 16 + place for at in zs]
    kv_z = [lax.rem(at, 4) * 2 + core for at in zs]

    def row(dx):
        return (z_hi * 16 + y * 4 + xs[dx % 4], kv)

    def column(dy):
        return (z_hi * 16 + ys[dy % 4] * 4 + x, kv)

    def line(dz):
        return (pb_z[dz % 8], kv_z[dz % 8])

    sibling = (pb, kv + 1 - 2 * core)
    sems = Sems()

    def copy(src, dst, peer):
        at = sems.take()
        return pltpu.make_async_remote_copy(
            src_ref=src, dst_ref=dst, send_sem=ssem.at[at], recv_sem=rsem.at[at],
            device_id=peer, device_id_type=MESH,
        )

    sent = []

    def start(copies):
        for one in copies:
            one.start()
            sent.append(one)

    def left():
        for one in sent:
            one.wait_send()
        sent.clear()

    def arrived(copies):
        for one in copies:
            one.wait_recv()

    barrier = pltpu.get_barrier_semaphore()
    peers = [line(d) for d in range(1, 8)] + [f(d) for f in (row, column) for d in (1, 2, 3)] + [sibling]
    for peer in peers:
        pl.semaphore_signal(barrier, inc=1, device_id=peer, device_id_type=MESH)
    qg[0, 0] = q_ref[...].T
    qg[0, 1] = g_ref[...].T
    kvg[0, 0, 0, 0] = k_ref[...]
    kvg[0, 0, 1, 0] = v_ref[...]
    pl.semaphore_wait(barrier, len(peers))

    k_row = {b: copy(kvg.at[0, 0, 0, 0], kvg.at[0, 0, 0, b], row(RING4[b])) for b in (1, 2, 3)}
    v_col = {t: copy(kvg.at[0, 0, 1, 0], kvg.at[t, 0, 1, 0], column(RING4[t])) for t in (1, 2, 3)}
    q_near = {i: copy(qg.at[0], qg.at[i], line(RING8[i])) for i in (3, 4, 1, 2)}
    k_col = {t: copy(kvg.at[0, 0, 0, 0], kvg.at[t, 0, 0, 0], column(RING4[t])) for t in (1, 2, 3)}
    v_row = {b: copy(kvg.at[0, 0, 1, 0], kvg.at[0, 0, 1, b], row(RING4[b])) for b in (1, 2, 3)}
    k_on = {t: copy(kvg.at[0, 0, 0, pl.ds(1, 3)], kvg.at[t, 0, 0, pl.ds(1, 3)], column(RING4[t])) for t in (1, 2, 3)}
    v_on = {
        t: [copy(kvg.at[t, 0, 1, 0], kvg.at[t, 0, 1, b], row(RING4[b])) for b in (1, 2, 3)] for t in (1, 2, 3)
    }
    q_on = {
        5: [copy(qg.at[3], qg.at[5], line(1))],
        6: [copy(qg.at[4], qg.at[6], line(-1))],
        7: [copy(qg.at[3, 0], qg.at[7, 0], line(2)), copy(qg.at[4, 1], qg.at[7, 1], line(-2))],
    }
    share = [copy(kvg.at[t, 0], kvg.at[t, 1], sibling) for t in range(4)]

    start([q_near[3], q_near[4]])
    start(k_row.values())
    start(v_col.values())
    start([q_near[1], q_near[2]])
    start(k_col.values())
    start(v_row.values())

    q_pos = []
    for i in range(ZQ):
        at_pb, at_kv = line(-RING8[i])
        q_pos.append(jnp.full((1, B), order_ref[at_kv * 32 + at_pb], jnp.int32))
    q_pos = jnp.concatenate(q_pos, axis=1)
    for t in range(4):
        for b in range(4):
            at_pb = z_hi * 16 + ys[-RING4[t] % 4] * 4 + xs[-RING4[b] % 4]
            for r in range(2):
                k_pos = order_ref[(kv + r * (1 - 2 * core)) * 32 + at_pb]
                bias[2 * t + r, b : b + 1, :] = jnp.where(k_pos > q_pos, BIG, 0.0)

    def quad(half, which):
        return jnp.concatenate([qg[4 * half + i, which] for i in range(4)], axis=1)

    def chunk(t, r, which):
        return kvg[t, r, which].reshape(KC, B)

    def unit(t, r, half, own=False):
        j = 2 * t + r
        at = slice(half * CH, (half + 1) * CH)
        s = dot(chunk(t, r, 0), quad(half, 0), 1, 0)
        dp = dot(chunk(t, r, 1), quad(half, 1), 1, 0)
        for b in range(4):
            here = slice(b * B, (b + 1) * B)
            sb, db = s[here], dp[here]
            if own and b == 0:
                lane = lax.broadcasted_iota(jnp.int32, (B, B), 1)
                sub = lax.broadcasted_iota(jnp.int32, (B, B), 0)
                first = sb[:, :B] + jnp.where(sub > lane, -BIG, 0.0)
                sb = jnp.concatenate([first, sb[:, B:]], axis=1)
            top = jnp.max(sb, axis=0, keepdims=True)
            p = jnp.exp2((sb - top) * log_scale)
            maxes[j, b : b + 1, at] = top
            totals[j, b : b + 1, at] = jnp.sum(p, axis=0, keepdims=True)
            deltas[j, b : b + 1, at] = jnp.sum(p * db, axis=0, keepdims=True)
            probs[j, here, at] = p.astype(BF16)
        dprobs[j, :, at] = dp

    def key_row(t):
        arrived([k_col[t], k_on[t]] + v_on[t])
        start([share[t]])

    arrived(k_row.values())
    start(k_on.values())
    arrived(v_col.values())
    for t in (1, 2, 3):
        start(v_on[t])
    arrived([q_near[3], q_near[4]])
    for i in (5, 6, 7):
        start(q_on[i])
    arrived(v_row.values())
    start([share[0]])
    arrived([q_near[1], q_near[2]])
    unit(0, 0, 0, own=True)
    arrived([share[0]])
    unit(0, 1, 0)
    for t in (1, 2, 3):
        key_row(t)
        unit(t, 0, 0)
    arrived([share[1]])
    unit(1, 1, 0)
    arrived(q_on[5] + q_on[6] + q_on[7])
    for t in range(4):
        unit(t, 0, 1)
    unit(0, 1, 1)
    unit(1, 1, 1)
    arrived([share[2], share[3]])
    for t in (2, 3):
        unit(t, 1, 0)
        unit(t, 1, 1)
    off = bias[...] > 0
    top = jnp.max(jnp.where(off, -BIG, maxes[...]), axis=(0, 1), keepdims=True)
    factor = jnp.where(off, 0.0, jnp.exp2((maxes[...] - top) * log_scale))
    total = jnp.maximum(jnp.sum(factor * totals[...], axis=(0, 1), keepdims=True), TINY)
    near = (top * log_scale + jnp.log2(total))[0]
    mean = (jnp.sum(factor * deltas[...], axis=(0, 1), keepdims=True) / total)[0]
    factors[...] = factor / total
    for i in range(ZQ):
        one = pl.ds(zs[-RING8[i] % 8], 1)
        st_send[0, one, :] = near[:, i * B : (i + 1) * B]
        st_send[1, one, :] = mean[:, i * B : (i + 1) * B]
    stats = [copy(st_send, st_recv.at[z], line(RING8[i])) for i in range(1, ZQ)]
    gathered = list(sent)
    sent.clear()
    start(stats[::-1])
    st_recv[z] = st_send[...]

    def turn(j):
        t, r = j // 2, j % 2
        kt[j] = chunk(t, r, 0).T
        vt[j] = chunk(t, r, 1).T

    for j in range(CHUNKS):
        turn(j)

    def scaled(j, at):
        p = probs[j, :, at].astype(F32).reshape(4, B, CH) * factors[j, :, at][:, None, :]
        return p.reshape(KC, CH)

    def attend(half):
        at = slice(half * CH, (half + 1) * CH)
        accum = jnp.zeros((B, CH), F32)
        for j in range(CHUNKS):
            accum += dot(vt[j], scaled(j, at).astype(BF16), 1, 0)
        accum = accum.astype(BF16)
        for i in range(4):
            o_send[4 * half + i] = accum[:, i * B : (i + 1) * B]

    attend(1)
    attend(0)
    o_copies = [copy(o_send.at[i], o_recv.at[i], line(-RING8[i])) for i in range(1, ZQ)]
    start(o_copies)
    o_recv[0] = o_send[0]

    for one in gathered:
        one.wait_send()
    arrived(stats)
    nears, means = st_recv[:, 0], st_recv[:, 1]
    top = jnp.max(nears, axis=0)
    lse = top + jnp.log2(jnp.sum(jnp.exp2(nears - top[None]), axis=0))
    rows[0:8, :] = lse
    rows[8:16, :] = jnp.sum(jnp.exp2(nears - lse[None]) * means, axis=0)

    def row_of(first):
        return jnp.concatenate([rows[pl.ds(first + zs[-RING8[i] % 8], 1), :] for i in range(ZQ)], axis=1)

    factors[...] = jnp.where(off, 0.0, jnp.exp2(maxes[...] * log_scale - row_of(0)[None]))
    rowdelta[...] = row_of(8)

    dq_copies = {i: copy(dq_send.at[i], dq_recv.at[i], line(-RING8[i])) for i in range(1, ZQ)}

    def weigh(j):
        for half in range(2):
            at = slice(half * CH, (half + 1) * CH)
            p = scaled(j, at)
            probs[j, :, at] = p.astype(BF16)
            dscores[j, :, at] = (p * (dprobs[j, :, at] - rowdelta[:, at])).astype(BF16)

    def query_grads(half):
        at = slice(half * CH, (half + 1) * CH)
        accum = jnp.zeros((B, CH), F32)
        for j in range(CHUNKS):
            accum += dot(kt[j], dscores[j, :, at], 1, 0)
        accum = (accum * scale).astype(BF16)
        for i in range(4 * half, 4 * half + 4):
            dq_send[i] = accum[:, (i - 4 * half) * B : (i - 4 * half + 1) * B]
        start([dq_copies[i] for i in range(4 * half + 3, 4 * half - 1, -1) if i])

    def whole(which):
        return jnp.concatenate([qg[i, which] for i in range(ZQ)], axis=1)

    def key_terms(t, r):
        j = 2 * t + r
        dk = dot(dscores[j], whole(0), 1, 1) * scale
        dv = dot(probs[j], whole(1), 1, 1)
        return dk.reshape(4, B, B), dv.reshape(4, B, B)

    swap = {t: copy(pre_send.at[t], pre_recv.at[t], sibling) for t in range(4)}
    dk_out = {t: copy(dk_row.at[t], dk_got.at[t], column(-RING4[t])) for t in (1, 2, 3)}
    dv_out = {
        t: [copy(dv_col.at[t, b], dv_got.at[t, b], row(-RING4[b])) for b in (1, 2, 3)] for t in range(4)
    }
    dk_end = {b: copy(dk_turn.at[b], dk_last.at[b], row(-RING4[b])) for b in (1, 2, 3)}
    dv_end = {t: copy(dv_turn.at[t], dv_last.at[t], column(-RING4[t])) for t in (1, 2, 3)}

    def send_half(t, *following):
        dk, dv = key_terms(t, 1)
        for j in following:
            weigh(j)
        pre_send[t, 0] = dk.astype(BF16)
        pre_send[t, 1] = dv.astype(BF16)
        start([swap[t]])

    def keep_half(t, *following):
        dk, dv = key_terms(t, 0)
        for j in following:
            weigh(j)
        part[t, 0] = dk
        part[t, 1] = dv

    def merge(t):
        arrived([swap[t]])
        dk_row[t] = (part[t, 0] + pre_recv[t, 0].astype(F32)).astype(BF16)
        dv_col[t] = (part[t, 1] + pre_recv[t, 1].astype(F32)).astype(BF16)
        if t:
            start([dk_out[t]])
        start(dv_out[t])

    def column_sum(t):
        arrived(dv_out[t])
        whole_sum = dv_col[t, 0].astype(F32)
        for b in (1, 2, 3):
            whole_sum += dv_got[t, b].astype(F32)
        return whole_sum

    def dv_pass(t):
        dv_turn[t] = column_sum(t).astype(BF16)
        start([dv_end[t]])

    weigh(7)
    send_half(3, 6)
    keep_half(3, 5)
    send_half(2, 4, 3, 2)
    merge(3)
    weigh(1)
    weigh(0)
    query_grads(1)
    query_grads(0)
    dq_recv[0] = dq_send[0]
    keep_half(2)
    merge(2)
    send_half(1)
    send_half(0)
    keep_half(1)
    merge(1)
    dv_pass(3)
    keep_half(0)
    merge(0)
    dv_pass(2)
    arrived(dk_out.values())
    turned = dk_row[0].astype(F32)
    for t in (1, 2, 3):
        turned += dk_got[t].astype(F32)
    dk_turn[...] = turned.astype(BF16)
    start([dk_end[b] for b in (3, 1, 2)])
    dv_pass(1)
    arrived(o_copies)
    out = jnp.zeros((B, B), F32)
    for i in range(ZQ):
        weight = jnp.exp2(st_recv[zs[RING8[i]], 0, pl.ds(z, 1), :] - rows[pl.ds(z, 1), :])
        out += o_recv[i].astype(F32) * weight
    out_ref[...] = out.astype(BF16).T
    arrived(dq_copies.values())
    dq_ref[...] = jnp.sum(dq_recv[...].astype(F32), axis=0).astype(BF16).T
    left()
    total_v = column_sum(0)
    arrived(dv_end.values())
    for t in (1, 2, 3):
        total_v += dv_last[t].astype(F32)
    dv_ref[...] = total_v.astype(BF16)
    total_k = dk_turn[0].astype(F32)
    arrived(dk_end.values())
    for b in (1, 2, 3):
        total_k += dk_last[b].astype(F32)
    dk_ref[...] = total_k.astype(BF16)


def finish(a_ref, b_ref, c_ref, d_ref, *outs):
    for src, dst in zip((a_ref, b_ref, c_ref, d_ref), outs):
        dst[...] = src[...]


def per_device(queries, keys, values, grad_out, block_order):
    vmem = pl.BlockSpec(memory_space=pltpu.VMEM)
    block = jax.ShapeDtypeStruct((B, B), BF16)
    parts = pl.pallas_call(
        kernel,
        out_shape=[block] * 4,
        in_specs=[vmem] * 4 + [pl.BlockSpec(memory_space=pltpu.SMEM)],
        out_specs=[vmem] * 4,
        scratch_shapes=[
            pltpu.VMEM((ZQ, 2, B, B), BF16),
            pltpu.VMEM((4, 2, 2, 4, B, B), BF16),
            pltpu.VMEM((CHUNKS, B, KC), BF16),
            pltpu.VMEM((CHUNKS, B, KC), BF16),
            pltpu.VMEM((CHUNKS, 4, NQ), F32),
            pltpu.VMEM((CHUNKS, 4, NQ), F32),
            pltpu.VMEM((CHUNKS, 4, NQ), F32),
            pltpu.VMEM((CHUNKS, 4, NQ), F32),
            pltpu.VMEM((CHUNKS, 4, NQ), F32),
            pltpu.VMEM((1, NQ), F32),
            pltpu.VMEM((16, B), F32),
            pltpu.VMEM((CHUNKS, KC, NQ), BF16),
            pltpu.VMEM((CHUNKS, KC, NQ), F32),
            pltpu.VMEM((CHUNKS, KC, NQ), BF16),
            pltpu.VMEM((2, 8, B), F32),
            pltpu.VMEM((ZQ, 2, 8, B), F32),
            pltpu.VMEM((ZQ, B, B), BF16),
            pltpu.VMEM((ZQ, B, B), BF16),
            pltpu.VMEM((ZQ, B, B), BF16),
            pltpu.VMEM((ZQ, B, B), BF16),
            pltpu.VMEM((4, 2, 4, B, B), BF16),
            pltpu.VMEM((4, 2, 4, B, B), BF16),
            pltpu.VMEM((4, 2, 4, B, B), F32),
            pltpu.VMEM((4, 4, B, B), BF16),
            pltpu.VMEM((4, 4, B, B), BF16),
            pltpu.VMEM((4, B, B), BF16),
            pltpu.VMEM((4, B, B), BF16),
            pltpu.VMEM((4, 4, B, B), BF16),
            pltpu.VMEM((4, 4, B, B), BF16),
            pltpu.VMEM((4, B, B), BF16),
            pltpu.VMEM((4, B, B), BF16),
            pltpu.SemaphoreType.DMA((SEMS,)),
            pltpu.SemaphoreType.DMA((SEMS,)),
        ],
        compiler_params=pltpu.CompilerParams(
            collective_id=0, has_side_effects=True, vmem_limit_bytes=60 * 2**20
        ),
        name="attention",
    )(queries, keys, values, grad_out, block_order)
    return pl.pallas_call(
        finish, out_shape=[block] * 4, in_specs=[vmem] * 4, out_specs=[vmem] * 4, name="finish"
    )(*parts)


def solution(mesh):
    spec = P(("kv", "pb"), None)
    return jax.shard_map(
        per_device, mesh=mesh, in_specs=(spec, spec, spec, spec, P()), out_specs=(spec,) * 4,
        check_vma=False,
    )
```

```python
import jax
import jax.numpy as jnp
from jax import lax
from jax.experimental import pallas as pl
from jax.experimental.pallas import tpu as pltpu
from jax.sharding import PartitionSpec as P

MESH = pl.DeviceIdType.MESH
F32 = jnp.float32
BF16 = jnp.bfloat16
BIG = 1e30
TINY = 1e-30
B = 128
ZQ = 8
NQ = ZQ * B
CHUNKS = 8
KC = 4 * B
CH = 4 * B
RING4 = (0, 1, 3, 2)
RING8 = (0, 1, 7, 2, 6, 3, 5, 4)


class Sems:
    def __init__(self):
        self.count = 0

    def take(self):
        self.count += 1
        return self.count - 1


SEMS = 82

def dot(left, right, left_dim, right_dim):
    return lax.dot_general(
        left, right, (((left_dim,), (right_dim,)), ((), ())), preferred_element_type=F32
    )


def kernel(
    q_ref, k_ref, v_ref, g_ref, order_ref,
    out_ref, dq_ref, dk_ref, dv_ref,
    qg, kvg, kt, vt, bias, maxes, totals, deltas, factors, rowdelta, rows, probs, dprobs, dscores,
    st_send, st_recv, o_send, o_recv, dq_send, dq_recv, pre_send, pre_recv, part,
    dk_row, dk_got, dk_turn, dk_last, dv_col, dv_got, dv_turn, dv_last,
    ssem, rsem,
):
    scale = B ** -0.5
    log_scale = scale * 1.4426950408889634
    pb, kv = lax.axis_index("pb"), lax.axis_index("kv")
    place = lax.rem(pb, 16)
    x, y = lax.rem(place, 4), place // 4
    z_hi = pb // 16
    z, core = z_hi * 4 + kv // 2, lax.rem(kv, 2)

    xs = [lax.rem(x + d, 4) for d in range(4)]
    ys = [lax.rem(y + d, 4) for d in range(4)]
    zs = [lax.rem(z + d, 8) for d in range(8)]
    pb_z = [at // 4 * 16 + place for at in zs]
    kv_z = [lax.rem(at, 4) * 2 + core for at in zs]

    def row(dx):
        return (z_hi * 16 + y * 4 + xs[dx % 4], kv)

    def column(dy):
        return (z_hi * 16 + ys[dy % 4] * 4 + x, kv)

    def line(dz):
        return (pb_z[dz % 8], kv_z[dz % 8])

    sibling = (pb, kv + 1 - 2 * core)
    sems = Sems()

    def copy(src, dst, peer):
        at = sems.take()
        return pltpu.make_async_remote_copy(
            src_ref=src, dst_ref=dst, send_sem=ssem.at[at], recv_sem=rsem.at[at],
            device_id=peer, device_id_type=MESH,
        )

    sent = []

    def start(copies):
        for one in copies:
            one.start()
            sent.append(one)

    def left():
        for one in sent:
            one.wait_send()
        sent.clear()

    def arrived(copies):
        for one in copies:
            one.wait_recv()

    barrier = pltpu.get_barrier_semaphore()
    peers = [line(d) for d in range(1, 8)] + [f(d) for f in (row, column) for d in (1, 2, 3)] + [sibling]
    for peer in peers:
        pl.semaphore_signal(barrier, inc=1, device_id=peer, device_id_type=MESH)
    qg[0, 0] = q_ref[...].T
    qg[0, 1] = g_ref[...].T
    kvg[0, 0, 0, 0] = k_ref[...]
    kvg[0, 0, 1, 0] = v_ref[...]
    pl.semaphore_wait(barrier, len(peers))

    k_row = {b: copy(kvg.at[0, 0, 0, 0], kvg.at[0, 0, 0, b], row(RING4[b])) for b in (1, 2, 3)}
    v_col = {t: copy(kvg.at[0, 0, 1, 0], kvg.at[t, 0, 1, 0], column(RING4[t])) for t in (1, 2, 3)}
    q_near = {i: copy(qg.at[0], qg.at[i], line(RING8[i])) for i in (3, 4, 1, 2)}
    k_col = {t: copy(kvg.at[0, 0, 0, 0], kvg.at[t, 0, 0, 0], column(RING4[t])) for t in (1, 2, 3)}
    v_row = {b: copy(kvg.at[0, 0, 1, 0], kvg.at[0, 0, 1, b], row(RING4[b])) for b in (1, 2, 3)}
    k_on = {t: copy(kvg.at[0, 0, 0, pl.ds(1, 3)], kvg.at[t, 0, 0, pl.ds(1, 3)], column(RING4[t])) for t in (1, 2, 3)}
    v_on = {
        t: [copy(kvg.at[t, 0, 1, 0], kvg.at[t, 0, 1, b], row(RING4[b])) for b in (1, 2, 3)] for t in (1, 2, 3)
    }
    q_on = {
        5: [copy(qg.at[3], qg.at[5], line(1))],
        6: [copy(qg.at[4], qg.at[6], line(-1))],
        7: [copy(qg.at[3, 0], qg.at[7, 0], line(2)), copy(qg.at[4, 1], qg.at[7, 1], line(-2))],
    }
    share = [copy(kvg.at[t, 0], kvg.at[t, 1], sibling) for t in range(4)]

    start([q_near[3], q_near[4]])
    start(k_row.values())
    start(v_col.values())
    start([q_near[1], q_near[2]])
    start(k_col.values())
    start(v_row.values())

    q_pos = []
    for i in range(ZQ):
        at_pb, at_kv = line(-RING8[i])
        q_pos.append(jnp.full((1, B), order_ref[at_kv * 32 + at_pb], jnp.int32))
    q_pos = jnp.concatenate(q_pos, axis=1)
    for t in range(4):
        for b in range(4):
            at_pb = z_hi * 16 + ys[-RING4[t] % 4] * 4 + xs[-RING4[b] % 4]
            for r in range(2):
                k_pos = order_ref[(kv + r * (1 - 2 * core)) * 32 + at_pb]
                bias[2 * t + r, b : b + 1, :] = jnp.where(k_pos > q_pos, BIG, 0.0)

    def quad(half, which):
        return jnp.concatenate([qg[4 * half + i, which] for i in range(4)], axis=1)

    def chunk(t, r, which):
        return kvg[t, r, which].reshape(KC, B)

    def unit(t, r, half, own=False):
        j = 2 * t + r
        at = slice(half * CH, (half + 1) * CH)
        s = dot(chunk(t, r, 0), quad(half, 0), 1, 0)
        dp = dot(chunk(t, r, 1), quad(half, 1), 1, 0)
        for b in range(4):
            here = slice(b * B, (b + 1) * B)
            sb, db = s[here], dp[here]
            if own and b == 0:
                lane = lax.broadcasted_iota(jnp.int32, (B, B), 1)
                sub = lax.broadcasted_iota(jnp.int32, (B, B), 0)
                first = sb[:, :B] + jnp.where(sub > lane, -BIG, 0.0)
                sb = jnp.concatenate([first, sb[:, B:]], axis=1)
            top = jnp.max(sb, axis=0, keepdims=True)
            p = jnp.exp2((sb - top) * log_scale)
            maxes[j, b : b + 1, at] = top
            totals[j, b : b + 1, at] = jnp.sum(p, axis=0, keepdims=True)
            deltas[j, b : b + 1, at] = jnp.sum(p * db, axis=0, keepdims=True)
            probs[j, here, at] = p.astype(BF16)
        dprobs[j, :, at] = dp

    def key_row(t):
        arrived([k_col[t], k_on[t]] + v_on[t])
        start([share[t]])

    arrived(k_row.values())
    start(k_on.values())
    arrived(v_col.values())
    for t in (1, 2, 3):
        start(v_on[t])
    arrived([q_near[3], q_near[4]])
    for i in (5, 6, 7):
        start(q_on[i])
    arrived(v_row.values())
    start([share[0]])
    arrived([q_near[1], q_near[2]])
    unit(0, 0, 0, own=True)
    arrived([share[0]])
    unit(0, 1, 0)
    for t in (1, 2, 3):
        if t == 3:
            arrived([share[1]])
            unit(1, 1, 0)
        key_row(t)
        unit(t, 0, 0)
    arrived(q_on[5] + q_on[6] + q_on[7])
    for t in range(4):
        unit(t, 0, 1)
    unit(0, 1, 1)
    unit(1, 1, 1)
    arrived([share[2], share[3]])
    for t in (2, 3):
        unit(t, 1, 0)
        unit(t, 1, 1)
    off = bias[...] > 0
    top = jnp.max(jnp.where(off, -BIG, maxes[...]), axis=(0, 1), keepdims=True)
    factor = jnp.where(off, 0.0, jnp.exp2((maxes[...] - top) * log_scale))
    total = jnp.maximum(jnp.sum(factor * totals[...], axis=(0, 1), keepdims=True), TINY)
    near = (top * log_scale + jnp.log2(total))[0]
    mean = (jnp.sum(factor * deltas[...], axis=(0, 1), keepdims=True) / total)[0]
    factors[...] = factor / total
    for i in range(ZQ):
        one = pl.ds(zs[-RING8[i] % 8], 1)
        st_send[0, one, :] = near[:, i * B : (i + 1) * B]
        st_send[1, one, :] = mean[:, i * B : (i + 1) * B]
    stats = [copy(st_send, st_recv.at[z], line(RING8[i])) for i in range(1, ZQ)]
    gathered = list(sent)
    sent.clear()
    start(stats[::-1])
    st_recv[z] = st_send[...]

    def turn(j):
        t, r = j // 2, j % 2
        kt[j] = chunk(t, r, 0).T
        vt[j] = chunk(t, r, 1).T

    for j in range(CHUNKS):
        turn(j)

    def scaled(j, at):
        p = probs[j, :, at].astype(F32).reshape(4, B, CH) * factors[j, :, at][:, None, :]
        return p.reshape(KC, CH)

    def attend(half):
        at = slice(half * CH, (half + 1) * CH)
        accum = jnp.zeros((B, CH), F32)
        for j in range(CHUNKS):
            accum += dot(vt[j], scaled(j, at).astype(BF16), 1, 0)
        accum = accum.astype(BF16)
        for i in range(4):
            o_send[4 * half + i] = accum[:, i * B : (i + 1) * B]

    attend(1)
    attend(0)
    o_copies = [copy(o_send.at[i], o_recv.at[i], line(-RING8[i])) for i in range(1, ZQ)]
    start(o_copies)
    o_recv[0] = o_send[0]

    for one in gathered:
        one.wait_send()
    arrived(stats)
    nears, means = st_recv[:, 0], st_recv[:, 1]
    top = jnp.max(nears, axis=0)
    lse = top + jnp.log2(jnp.sum(jnp.exp2(nears - top[None]), axis=0))
    rows[0:8, :] = lse
    rows[8:16, :] = jnp.sum(jnp.exp2(nears - lse[None]) * means, axis=0)

    def row_of(first):
        return jnp.concatenate([rows[pl.ds(first + zs[-RING8[i] % 8], 1), :] for i in range(ZQ)], axis=1)

    factors[...] = jnp.where(off, 0.0, jnp.exp2(maxes[...] * log_scale - row_of(0)[None]))
    rowdelta[...] = row_of(8)

    dq_copies = {i: copy(dq_send.at[i], dq_recv.at[i], line(-RING8[i])) for i in range(1, ZQ)}

    def weigh(j):
        for half in range(2):
            at = slice(half * CH, (half + 1) * CH)
            p = scaled(j, at)
            probs[j, :, at] = p.astype(BF16)
            dscores[j, :, at] = (p * (dprobs[j, :, at] - rowdelta[:, at])).astype(BF16)

    def query_grads(half):
        at = slice(half * CH, (half + 1) * CH)
        accum = jnp.zeros((B, CH), F32)
        for j in range(CHUNKS):
            accum += dot(kt[j], dscores[j, :, at], 1, 0)
        accum = (accum * scale).astype(BF16)
        for i in range(4 * half, 4 * half + 4):
            dq_send[i] = accum[:, (i - 4 * half) * B : (i - 4 * half + 1) * B]
        start([dq_copies[i] for i in range(4 * half + 3, 4 * half - 1, -1) if i])

    def whole(which):
        return jnp.concatenate([qg[i, which] for i in range(ZQ)], axis=1)

    def key_terms(t, r):
        j = 2 * t + r
        dk = dot(dscores[j], whole(0), 1, 1) * scale
        dv = dot(probs[j], whole(1), 1, 1)
        return dk.reshape(4, B, B), dv.reshape(4, B, B)

    swap = {t: copy(pre_send.at[t], pre_recv.at[t], sibling) for t in range(4)}
    dk_out = {t: copy(dk_row.at[t], dk_got.at[t], column(-RING4[t])) for t in (1, 2, 3)}
    dv_out = {
        t: [copy(dv_col.at[t, b], dv_got.at[t, b], row(-RING4[b])) for b in (1, 2, 3)] for t in range(4)
    }
    dk_end = {b: copy(dk_turn.at[b], dk_last.at[b], row(-RING4[b])) for b in (1, 2, 3)}
    dv_end = {t: copy(dv_turn.at[t], dv_last.at[t], column(-RING4[t])) for t in (1, 2, 3)}

    def send_half(t, *following):
        dk, dv = key_terms(t, 1)
        for j in following:
            weigh(j)
        pre_send[t, 0] = dk.astype(BF16)
        pre_send[t, 1] = dv.astype(BF16)
        start([swap[t]])

    def keep_half(t, *following):
        dk, dv = key_terms(t, 0)
        for j in following:
            weigh(j)
        part[t, 0] = dk
        part[t, 1] = dv

    def merge(t):
        arrived([swap[t]])
        dk_row[t] = (part[t, 0] + pre_recv[t, 0].astype(F32)).astype(BF16)
        dv_col[t] = (part[t, 1] + pre_recv[t, 1].astype(F32)).astype(BF16)
        if t:
            start([dk_out[t]])
        start(dv_out[t])

    def column_sum(t):
        arrived(dv_out[t])
        whole_sum = dv_col[t, 0].astype(F32)
        for b in (1, 2, 3):
            whole_sum += dv_got[t, b].astype(F32)
        return whole_sum

    def dv_pass(t):
        dv_turn[t] = column_sum(t).astype(BF16)
        start([dv_end[t]])

    weigh(7)
    send_half(3, 6)
    keep_half(3, 5)
    send_half(2, 4, 3, 2)
    merge(3)
    weigh(1)
    weigh(0)
    query_grads(1)
    query_grads(0)
    dq_recv[0] = dq_send[0]
    keep_half(2)
    merge(2)
    send_half(1)
    send_half(0)
    keep_half(1)
    merge(1)
    dv_pass(3)
    keep_half(0)
    merge(0)
    dv_pass(2)
    arrived(dk_out.values())
    turned = dk_row[0].astype(F32)
    for t in (1, 2, 3):
        turned += dk_got[t].astype(F32)
    dk_turn[...] = turned.astype(BF16)
    start([dk_end[b] for b in (3, 1, 2)])
    dv_pass(1)
    arrived(o_copies)
    out = jnp.zeros((B, B), F32)
    for i in range(ZQ):
        weight = jnp.exp2(st_recv[zs[RING8[i]], 0, pl.ds(z, 1), :] - rows[pl.ds(z, 1), :])
        out += o_recv[i].astype(F32) * weight
    out_ref[...] = out.astype(BF16).T
    arrived(dq_copies.values())
    dq_ref[...] = jnp.sum(dq_recv[...].astype(F32), axis=0).astype(BF16).T
    left()
    total_v = column_sum(0)
    arrived(dv_end.values())
    for t in (1, 2, 3):
        total_v += dv_last[t].astype(F32)
    dv_ref[...] = total_v.astype(BF16)
    total_k = dk_turn[0].astype(F32)
    arrived(dk_end.values())
    for b in (1, 2, 3):
        total_k += dk_last[b].astype(F32)
    dk_ref[...] = total_k.astype(BF16)


def finish(a_ref, b_ref, c_ref, d_ref, *outs):
    for src, dst in zip((a_ref, b_ref, c_ref, d_ref), outs):
        dst[...] = src[...]


def per_device(queries, keys, values, grad_out, block_order):
    vmem = pl.BlockSpec(memory_space=pltpu.VMEM)
    block = jax.ShapeDtypeStruct((B, B), BF16)
    parts = pl.pallas_call(
        kernel,
        out_shape=[block] * 4,
        in_specs=[vmem] * 4 + [pl.BlockSpec(memory_space=pltpu.SMEM)],
        out_specs=[vmem] * 4,
        scratch_shapes=[
            pltpu.VMEM((ZQ, 2, B, B), BF16),
            pltpu.VMEM((4, 2, 2, 4, B, B), BF16),
            pltpu.VMEM((CHUNKS, B, KC), BF16),
            pltpu.VMEM((CHUNKS, B, KC), BF16),
            pltpu.VMEM((CHUNKS, 4, NQ), F32),
            pltpu.VMEM((CHUNKS, 4, NQ), F32),
            pltpu.VMEM((CHUNKS, 4, NQ), F32),
            pltpu.VMEM((CHUNKS, 4, NQ), F32),
            pltpu.VMEM((CHUNKS, 4, NQ), F32),
            pltpu.VMEM((1, NQ), F32),
            pltpu.VMEM((16, B), F32),
            pltpu.VMEM((CHUNKS, KC, NQ), BF16),
            pltpu.VMEM((CHUNKS, KC, NQ), F32),
            pltpu.VMEM((CHUNKS, KC, NQ), BF16),
            pltpu.VMEM((2, 8, B), F32),
            pltpu.VMEM((ZQ, 2, 8, B), F32),
            pltpu.VMEM((ZQ, B, B), BF16),
            pltpu.VMEM((ZQ, B, B), BF16),
            pltpu.VMEM((ZQ, B, B), BF16),
            pltpu.VMEM((ZQ, B, B), BF16),
            pltpu.VMEM((4, 2, 4, B, B), BF16),
            pltpu.VMEM((4, 2, 4, B, B), BF16),
            pltpu.VMEM((4, 2, 4, B, B), F32),
            pltpu.VMEM((4, 4, B, B), BF16),
            pltpu.VMEM((4, 4, B, B), BF16),
            pltpu.VMEM((4, B, B), BF16),
            pltpu.VMEM((4, B, B), BF16),
            pltpu.VMEM((4, 4, B, B), BF16),
            pltpu.VMEM((4, 4, B, B), BF16),
            pltpu.VMEM((4, B, B), BF16),
            pltpu.VMEM((4, B, B), BF16),
            pltpu.SemaphoreType.DMA((SEMS,)),
            pltpu.SemaphoreType.DMA((SEMS,)),
        ],
        compiler_params=pltpu.CompilerParams(
            collective_id=0, has_side_effects=True, vmem_limit_bytes=60 * 2**20
        ),
        name="attention",
    )(queries, keys, values, grad_out, block_order)
    return pl.pallas_call(
        finish, out_shape=[block] * 4, in_specs=[vmem] * 4, out_specs=[vmem] * 4, name="finish"
    )(*parts)


def solution(mesh):
    spec = P(("kv", "pb"), None)
    return jax.shard_map(
        per_device, mesh=mesh, in_specs=(spec, spec, spec, spec, P()), out_specs=(spec,) * 4,
        check_vma=False,
    )
```
